512 devices in a mesh: ctx: 32 (over y, z_hi), head: 16 (over z_lo, x, core).
Axes of the slice: x: 4, y: 8, z: 8 (z_hi: 4, z_lo: 2; z = z_hi * 2 + z_lo), core: 2. Of those that a mesh axis runs over, the one named last changes fastest.
Arguments:
- block_owner: int32 [64], P('ctx'), may hold values from 0 to 63, each once
- query_nope: bfloat16 [4096, 8192], P('ctx', 'head'), may hold values from -6 to 6
- query_rope: bfloat16 [4096, 4096], P('ctx', 'head'), may hold values from -90 to 90
- latent_cache: bfloat16 [4096, 576], P('ctx'), may hold values from -6 to 6, as said below
- key_up_weight: bfloat16 [512, 8192], P(None, 'head'), may hold values from -0.25 to 0.25
- value_up_weight: bfloat16 [512, 8192], P(None, 'head'), may hold values from -0.25 to 0.25
- saved_output: bfloat16 [4096, 32768], P('ctx', 'head'), may hold values from -4 to 4
- output_grad: bfloat16 [4096, 8192], P('ctx', 'head'), may hold values from -6 to 6
Outputs:
- grad_query_nope: bfloat16 [4096, 8192], P('ctx', 'head')
- grad_query_rope: bfloat16 [4096, 4096], P('ctx', 'head')
- grad_latent: bfloat16 [4096, 512], P('ctx')
- grad_key_up: float32 [512, 8192], P(None, 'head')
- grad_value_up: float32 [512, 8192], P(None, 'head')
The draws below stay inside these ranges and needn't reach their ends.
Inputs may be any that keep to these rules, and one draw needn't show every extreme that they name: `latent_cache`: in every row the first 512 entries are the latent and the last 64 the rotary key.
All inputs are finite; a program needn't handle non-finite values.
Results may differ from the reference program's by a relative error of at most 0.03.
Values may be sent and summed in bfloat16 or wider, within the bound.
A program may use at most 64 MiB of HBM per device.

```python
import jax
import jax.numpy as jnp
from jax import lax

LATENT = 512
ROPE = 64
NOPE = 128
HEAD_DEV = 4
TOK_DEV = 128
HEADS = 64
TOKENS = 4096
BLOCKS = 64
N_CTX = 32
N_HEAD = 16


def rope_base(key):
    total_rows = TOK_DEV * N_CTX
    return jnp.clip(jax.random.normal(key, (total_rows, ROPE), jnp.float32), -6.0, 6.0)


def draw_latent_cache(key, part):
    base = rope_base(key)
    key = jax.random.fold_in(key, 5)
    total_rows = TOK_DEV * N_CTX
    latent = jnp.clip(jax.random.normal(key, (total_rows, LATENT), jnp.float32), -6.0, 6.0)
    rope_part = base
    return jnp.concatenate([latent, rope_part], 1).astype(jnp.bfloat16)


def draw_query_rope(key, part):
    key = jax.random.fold_in(key, 7)
    total_rows = TOK_DEV * N_CTX
    heads_total = HEAD_DEV * N_HEAD
    values = jnp.clip(jax.random.normal(key, (total_rows, heads_total, ROPE), jnp.float32), -6.0, 6.0)
    return values.reshape(total_rows, heads_total * ROPE).astype(jnp.bfloat16)


def block_scale(own_key, extent, pieces, low, top_value):
    level, own = 1.0, jax.random.fold_in(own_key, 6)
    for position, shards_of in pieces:
        draws = jnp.exp(jax.random.uniform(jax.random.fold_in(own, position), (shards_of,), jnp.float32, low / len(pieces), top_value / len(pieces)))
        level = level * jnp.repeat(draws, extent[position] // shards_of).reshape([-1 if axis == position else 1 for axis in range(len(extent))])
    return level


def gaussian(stream_key, shape, width, most, shards=(), kind=jnp.bfloat16):
    array = width * jax.random.normal(stream_key, shape, jnp.float32)
    if shards:
        array = array * block_scale(stream_key, shape, shards, -0.22, 0.18)
    return jnp.clip(array, -most, most).astype(kind)


def setup_inputs(seed: int = 0) -> dict:
    arg_keys = jax.random.split(jax.random.key(seed), 9)
    block_owner = jax.random.permutation(arg_keys[0], BLOCKS).astype(jnp.int32)
    query_nope = gaussian(arg_keys[1], (TOKENS, HEADS * NOPE), 1.0, 6.0, ((0, 32), (1, 16)))
    query_rope = draw_query_rope(jax.random.fold_in(arg_keys[8], 71), 0)
    latent_cache = draw_latent_cache(jax.random.fold_in(arg_keys[8], 71), 0)
    key_up_weight = gaussian(arg_keys[4], (LATENT, HEADS * NOPE), LATENT ** -0.5, 0.25, ((1, 16),))
    value_up_weight = gaussian(arg_keys[5], (LATENT, HEADS * NOPE), LATENT ** -0.5, 0.25, ((1, 16),))
    saved_output = gaussian(arg_keys[6], (TOKENS, HEADS * LATENT), 0.3, 4.0, ((0, 32), (1, 16)))
    output_grad = gaussian(arg_keys[7], (TOKENS, HEADS * NOPE), 1.0, 6.0, ((0, 32), (1, 16)))
    return {"block_owner": block_owner, "query_nope": query_nope, "query_rope": query_rope, "latent_cache": latent_cache, "key_up_weight": key_up_weight, "value_up_weight": value_up_weight, "saved_output": saved_output, "output_grad": output_grad}


def sequence_positions(block_owner):
    half_rows = TOK_DEV // 2
    offsets = jnp.arange(half_rows, dtype=jnp.int32)
    return (block_owner[:, None] * half_rows + offsets[None, :]).reshape(-1).astype(jnp.int32)


def reference(block_owner, query_nope, query_rope, latent_cache, key_up_weight, value_up_weight, saved_output, output_grad):
    softmax_scale = (NOPE + ROPE) ** -0.5
    key_positions = sequence_positions(block_owner)
    group_rows = HEAD_DEV * TOK_DEV

    def one_group(carried, device_index):
        latent_total, key_total, value_total = carried
        ctx_index = (device_index // N_HEAD).astype(jnp.int32)
        head_index = (device_index % N_HEAD).astype(jnp.int32)
        row_start = ctx_index * TOK_DEV
        zero_index = jnp.zeros((), jnp.int32)
        query_split = lax.dynamic_slice(query_nope, (row_start, head_index * HEAD_DEV * NOPE), (TOK_DEV, HEAD_DEV * NOPE)).reshape(TOK_DEV, HEAD_DEV, NOPE)
        rotary = lax.dynamic_slice(query_rope, (row_start, head_index * HEAD_DEV * ROPE), (TOK_DEV, HEAD_DEV * ROPE)).reshape(TOK_DEV, HEAD_DEV, ROPE)
        key_weight = lax.dynamic_slice(key_up_weight, (zero_index, head_index * HEAD_DEV * NOPE), (LATENT, HEAD_DEV * NOPE)).reshape(LATENT, HEAD_DEV, NOPE)
        value_weight = lax.dynamic_slice(value_up_weight, (zero_index, head_index * HEAD_DEV * NOPE), (LATENT, HEAD_DEV * NOPE)).reshape(LATENT, HEAD_DEV, NOPE)
        saved_split = lax.dynamic_slice(saved_output, (row_start, head_index * HEAD_DEV * LATENT), (TOK_DEV, HEAD_DEV * LATENT)).reshape(TOK_DEV, HEAD_DEV, LATENT)
        output_split = lax.dynamic_slice(output_grad, (row_start, head_index * HEAD_DEV * NOPE), (TOK_DEV, HEAD_DEV * NOPE)).reshape(TOK_DEV, HEAD_DEV, NOPE)

        absorbed = jnp.einsum("thd,lhd->htl", query_split.astype(jnp.float32), key_weight.astype(jnp.float32)).astype(jnp.bfloat16).reshape(group_rows, LATENT)
        rotary_rows = rotary.transpose(1, 0, 2).reshape(group_rows, ROPE)
        queries = jnp.concatenate([absorbed, rotary_rows], 1)
        query_positions = jnp.tile(lax.dynamic_slice_in_dim(key_positions, row_start, TOK_DEV, 0), HEAD_DEV)
        visible = key_positions[None, :] <= query_positions[:, None]
        raw_scores = jnp.dot(queries, latent_cache.T, preferred_element_type=jnp.float32) * softmax_scale
        masked = jnp.where(visible, raw_scores, -1e30)
        row_max = jnp.max(masked, 1)
        weights = jnp.where(visible, jnp.exp(masked - row_max[:, None]), 0.0)
        log_norm = row_max + jnp.log(jnp.sum(weights, 1))
        probabilities = jnp.where(visible, jnp.exp(masked - log_norm[:, None]), 0.0)
        probs_low = probabilities.astype(jnp.bfloat16)

        latent_grad_out = jnp.einsum("thd,lhd->htl", output_split.astype(jnp.float32), value_weight.astype(jnp.float32)).astype(jnp.bfloat16).reshape(group_rows, LATENT)
        saved_rows = saved_split.transpose(1, 0, 2).reshape(group_rows, LATENT)
        row_delta = jnp.sum(latent_grad_out.astype(jnp.float32) * saved_rows.astype(jnp.float32), 1)
        prob_grad = jnp.dot(latent_grad_out, latent_cache[:, :LATENT].T, preferred_element_type=jnp.float32)
        score_grad = (probabilities * (prob_grad - row_delta[:, None]) * softmax_scale).astype(jnp.bfloat16)
        query_grad_full = jnp.dot(score_grad, latent_cache, preferred_element_type=jnp.float32)
        absorbed_grad = query_grad_full[:, :LATENT].astype(jnp.bfloat16).reshape(HEAD_DEV, TOK_DEV, LATENT)
        rope_grad = query_grad_full[:, LATENT:].astype(jnp.bfloat16).reshape(HEAD_DEV, TOK_DEV, ROPE).transpose(1, 0, 2).reshape(TOK_DEV, HEAD_DEV * ROPE)
        nope_grad = jnp.einsum("htl,lhd->thd", absorbed_grad.astype(jnp.float32), key_weight.astype(jnp.float32)).astype(jnp.bfloat16).reshape(TOK_DEV, HEAD_DEV * NOPE)
        key_part = jnp.einsum("htl,thd->lhd", absorbed_grad.astype(jnp.float32), query_split.astype(jnp.float32)).reshape(LATENT, HEAD_DEV * NOPE)
        value_part = jnp.einsum("thl,thd->lhd", saved_split.astype(jnp.float32), output_split.astype(jnp.float32)).reshape(LATENT, HEAD_DEV * NOPE)
        latent_partial = (jnp.dot(score_grad.T, absorbed, preferred_element_type=jnp.float32) + jnp.dot(probs_low.T, latent_grad_out, preferred_element_type=jnp.float32)).astype(jnp.bfloat16)

        latent_total = latent_total + latent_partial.astype(jnp.float32)
        column = head_index * HEAD_DEV * NOPE
        key_total = lax.dynamic_update_slice(key_total, lax.dynamic_slice(key_total, (zero_index, column), (LATENT, HEAD_DEV * NOPE)) + key_part, (zero_index, column))
        value_total = lax.dynamic_update_slice(value_total, lax.dynamic_slice(value_total, (zero_index, column), (LATENT, HEAD_DEV * NOPE)) + value_part, (zero_index, column))
        return (latent_total, key_total, value_total), (nope_grad, rope_grad)

    heads_total = HEAD_DEV * N_HEAD
    start_state = (jnp.zeros((TOKENS, LATENT), jnp.float32), jnp.zeros((LATENT, heads_total * NOPE), jnp.float32), jnp.zeros((LATENT, heads_total * NOPE), jnp.float32))
    final_state, stacked = lax.scan(one_group, start_state, jnp.arange(N_CTX * N_HEAD, dtype=jnp.int32))
    latent_total, key_total, value_total = final_state
    nope_stack, rope_stack = stacked
    grad_query_nope = nope_stack.reshape(N_CTX, N_HEAD, TOK_DEV, HEAD_DEV * NOPE).transpose(0, 2, 1, 3).reshape(TOKENS, heads_total * NOPE)
    grad_query_rope = rope_stack.reshape(N_CTX, N_HEAD, TOK_DEV, HEAD_DEV * ROPE).transpose(0, 2, 1, 3).reshape(TOKENS, heads_total * ROPE)
    return grad_query_nope, grad_query_rope, latent_total.astype(jnp.bfloat16), key_total, value_total
```

```python
import functools
import math

import jax
import jax.numpy as jnp
from jax import lax
from jax.experimental import pallas as pl
from jax.experimental.pallas import tpu as pltpu
from jax.sharding import PartitionSpec as P

LATENT = 512
ROPE = 64
NOPE = 128
NY, NZH, NX = 8, 4, 4
NZ = 2 * NZH
BLOCKS = 64
WIDE = LATENT + ROPE + BLOCKS
TOK = 128
CHUNK = 512
HIDDEN = -1e30
BF16 = jnp.bfloat16
F32 = jnp.float32
VMEM_LIMIT = 58 * 1024 * 1024


def place():
    ctx, head = lax.axis_index("ctx"), lax.axis_index("head")
    y, zh = ctx // NZH, lax.rem(ctx, NZH)
    zl = head // (2 * NX)
    x = lax.rem(head // 2, NX)
    core = lax.rem(head, 2)
    return y, zh, zl, x, core


def device(y, zh, zl, x, core):
    return (y * NZH + zh, zl * (2 * NX) + x * 2 + core)


def copy_to(src, dst, send_sem, recv_sem, target):
    return pltpu.make_async_remote_copy(
        src_ref=src,
        dst_ref=dst,
        send_sem=send_sem,
        recv_sem=recv_sem,
        device_id=target,
        device_id_type=pl.DeviceIdType.MESH,
    )


def greet(peers):
    barrier = pltpu.get_barrier_semaphore()
    for peer in peers:
        pl.semaphore_signal(barrier, inc=1, device_id=peer, device_id_type=pl.DeviceIdType.MESH)
    pl.semaphore_wait(barrier, len(peers))


def wrap(index, size):
    return lax.rem(index + 2 * size, size)


def gather_kernel(
    owner, latent, keys, near_send, near_recv, y_send, y_recv, z_send, z_recv, core_send, core_recv
):
    y, zh, zl, x, core = place()
    turn = 1 - 2 * core
    z = 2 * zh + zl
    sibling = device(y, zh, zl, x, 1 - core)
    y_peers = [device(wrap(y + d, NY), zh, zl, x, core) for d in range(1, NY)]
    zh_peers = [device(y, wrap(zh + d, NZH), zl, x, core) for d in range(1, NZH)]

    def z_device(where):
        return device(y, where // 2, lax.rem(where, 2), x, core)

    ring_peers = [z_device(wrap(z + 1, NZ)), z_device(wrap(z - 1, NZ))]

    column = lax.broadcasted_iota(jnp.int32, (16, BLOCKS), 1)
    for half in range(2):
        mark = jnp.where(column == owner[half], 1.0, 0.0).astype(BF16)
        for part in range(2):
            for low in range(2):
                start = half * 64 + part * 32 + low * 16
                keys[y, zh, half, part, low, :, : LATENT + ROPE] = latent[pl.ds(start, 16), :]
                keys[y, zh, half, part, low, :, LATENT + ROPE :] = mark

    greet([sibling] + y_peers + zh_peers + ring_peers)

    first = []
    for d in range(1, NZH):
        region = keys.at[y, zh, core, 0]
        first.append(copy_to(region, region, near_send.at[d - 1], near_recv.at[d - 1], zh_peers[d - 1]))
    for d in range(1, NY):
        region = keys.at[y, zh, core, 1, zl]
        slot = NZH - 1 + d - 1
        first.append(copy_to(region, region, near_send.at[slot], near_recv.at[slot], y_peers[d - 1]))
    for copy in first:
        copy.start()

    passed = []

    def pass_on(region):
        slot = len(passed)
        copy = copy_to(region, region, core_send.at[slot], core_recv.at[slot], sibling)
        copy.start()
        other = 1 - core
        passed.append(copy)

    half_y, half_z = NZH // 2, NY // 2
    y_next = device(wrap(y + turn, NY), zh, zl, x, core)
    z_next = z_device(wrap(z + turn, NZ))

    def y_copy(step, sub):
        where = wrap(y - turn * step, NY)
        region = keys.at[where, pl.ds(sub * half_y, half_y), core, 0]
        return copy_to(region, region, y_send.at[step, sub], y_recv.at[step, sub], y_next)

    def y_arrived(step, sub):
        where = wrap(y - turn * (step + 1), NY)
        region = keys.at[where, pl.ds(sub * half_y, half_y), core, 0]
        return copy_to(region, region, y_send.at[step, sub], y_recv.at[step, sub], y_next)

    def z_region(where, sub):
        return keys.at[pl.ds(sub * half_z, half_z), where // 2, core, 1, lax.rem(where, 2)]

    def z_copy(step, sub):
        region = z_region(wrap(z - turn * step, NZ), sub)
        return copy_to(region, region, z_send.at[step, sub], z_recv.at[step, sub], z_next)

    def z_arrived(step, sub):
        region = z_region(wrap(z - turn * (step + 1), NZ), sub)
        return copy_to(region, region, z_send.at[step, sub], z_recv.at[step, sub], z_next)

    for d in range(1, NZH):
        region = keys.at[y, wrap(zh - d, NZH), core, 0]
        copy_to(region, region, near_send.at[d - 1], near_recv.at[d - 1], zh_peers[d - 1]).wait_recv()
    for sub in range(2):
        y_copy(0, sub).start()
    for d in range(1, NY):
        region = keys.at[wrap(y - d, NY), zh, core, 1, zl]
        slot = NZH - 1 + d - 1
        copy_to(region, region, near_send.at[slot], near_recv.at[slot], y_peers[d - 1]).wait_recv()
    for sub in range(2):
        z_copy(0, sub).start()
    for d in range(1, NZH):
        pass_on(keys.at[y, wrap(zh - d, NZH), core, 0])
    pass_on(keys.at[:, zh, core, 1, zl])
    for copy in first:
        copy.wait_send()

    for step in range(max(NY, NZ) - 1):
        for sub in range(2):
            if step < NY - 1:
                y_arrived(step, sub).wait_recv()
                if step + 1 < NY - 1:
                    y_copy(step + 1, sub).start()
            if step < NZ - 1:
                z_arrived(step, sub).wait_recv()
                if step + 1 < NZ - 1:
                    z_copy(step + 1, sub).start()
        if step < NY - 1:
            pass_on(keys.at[wrap(y - turn * (step + 1), NY), :, core, 0])
        if step < NZ - 1:
            where = wrap(z - turn * (step + 1), NZ)
            pass_on(keys.at[:, where // 2, core, 1, lax.rem(where, 2)])
    for step in range(NY - 1):
        for sub in range(2):
            y_copy(step, sub).wait_send()
    for step in range(NZ - 1):
        for sub in range(2):
            z_copy(step, sub).wait_send()
    for copy in passed:
        copy.wait_send()
    slot = 0
    other = 1 - core
    arrivals = [keys.at[y, wrap(zh - d, NZH), other, 0] for d in range(1, NZH)]
    arrivals.append(keys.at[:, zh, other, 1, zl])
    for step in range(max(NY, NZ) - 1):
        if step < NY - 1:
            arrivals.append(keys.at[wrap(y + turn * (step + 1), NY), :, other, 0])
        if step < NZ - 1:
            where = wrap(z + turn * (step + 1), NZ)
            arrivals.append(keys.at[:, where // 2, other, 1, lax.rem(where, 2)])
    for slot, region in enumerate(arrivals):
        copy_to(region, region, core_send.at[slot], core_recv.at[slot], sibling).wait_recv()


def gather_keys(owner, latent):
    passes = NZH - 1 + 1 + (NY - 1) + (NZ - 1)
    near = NZH - 1 + NY - 1
    dma = pltpu.SemaphoreType.DMA
    return pl.pallas_call(
        gather_kernel,
        out_shape=jax.ShapeDtypeStruct((NY, NZH, 2, 2, 2, 16, WIDE), BF16),
        in_specs=[
            pl.BlockSpec(memory_space=pltpu.SMEM),
            pl.BlockSpec(memory_space=pltpu.VMEM),
        ],
        out_specs=pl.BlockSpec(memory_space=pltpu.VMEM),
        scratch_shapes=[
            dma((near,)),
            dma((near,)),
            dma((NY - 1, 2)),
            dma((NY - 1, 2)),
            dma((NZ - 1, 2)),
            dma((NZ - 1, 2)),
            dma((passes,)),
            dma((passes,)),
        ],
        compiler_params=pltpu.CompilerParams(
            collective_id=0, has_side_effects=True, vmem_limit_bytes=VMEM_LIMIT
        ),
        name="gather_keys",
    )(owner, latent)


def dot(left, right):
    return jnp.dot(left, right, preferred_element_type=F32)


def dot_nt(left, right):
    return lax.dot_general(left, right, (((1,), (1,)), ((), ())), preferred_element_type=F32)


def dot_tn(left, right):
    return lax.dot_general(left, right, (((0,), (0,)), ((), ())), preferred_element_type=F32)


def attention_kernel(
    owner,
    keys,
    query_nope,
    query_rope,
    key_weight,
    value_weight,
    saved,
    output_grad,
    grad_nope,
    grad_rope,
    latent_part,
    weight_part,
    query_t,
    absorbed,
    grad_out_t,
    grad_out,
    delta,
    weights,
    prob_grad,
    tops,
    sums,
    query_grad,
):
    heads = query_nope.shape[1] // NOPE
    rows = heads * TOK
    scale = (NOPE + ROPE) ** -0.5
    log2_scale = scale * math.log2(math.e)
    chunks = keys.shape[0] // CHUNK
    own = lax.axis_index("ctx")

    rope_t = query_rope[...].astype(F32).T.astype(BF16)
    block = lax.broadcasted_iota(jnp.int32, (BLOCKS, TOK), 0)
    token = lax.broadcasted_iota(jnp.int32, (BLOCKS, TOK), 1)
    limit = jnp.where(token < TOK // 2, owner[0], owner[1])
    bias = jnp.where(block <= limit, 0.0, HIDDEN).astype(BF16)
    for h in range(heads):
        cols = slice(h * NOPE, (h + 1) * NOPE)
        span = slice(h * TOK, (h + 1) * TOK)
        query, weight = query_nope[:, cols], key_weight[:, cols]
        absorbed[span, :] = dot_nt(query, weight).astype(BF16)
        query_t[:LATENT, span] = dot_nt(weight, query).astype(BF16)
        query_t[LATENT : LATENT + ROPE, span] = rope_t[h * ROPE : (h + 1) * ROPE, :]
        query_t[LATENT + ROPE :, span] = bias
        out, weight = output_grad[:, cols], value_weight[:, cols]
        grads = dot_nt(out, weight).astype(BF16)
        grad_out[span, :] = grads
        grad_out_t[:, span] = dot_nt(weight, out).astype(BF16)
        held = saved[:, h * LATENT : (h + 1) * LATENT]
        product = grads.astype(F32) * held.astype(F32)
        delta[:, span] = jnp.sum(product.T, axis=0, keepdims=True)
        weight_part[LATENT:, cols] = dot_tn(held, out).astype(BF16)

    def score(index, carry):
        span = pl.ds(pl.multiple_of(index * CHUNK, CHUNK), CHUNK)
        weights[span, :] = dot(keys[span, :], query_t[...])
        prob_grad[span, :] = dot(keys[span, :LATENT], grad_out_t[...])

        @pl.when(index == own // (CHUNK // TOK))
        def _():
            mine = pl.ds(pl.multiple_of(own * TOK, TOK), TOK)
            key_row = lax.broadcasted_iota(jnp.int32, (TOK, rows), 0)
            query_row = lax.rem(lax.broadcasted_iota(jnp.int32, (TOK, rows), 1), TOK)
            half = TOK // 2
            later = (key_row // half == query_row // half) & (key_row > query_row)
            weights[mine, :] = jnp.where(later, HIDDEN, weights[mine, :])

        raw = weights[span, :]
        top = jnp.max(raw, axis=0, keepdims=True)
        raised = jnp.exp2((raw - top) * log2_scale)
        weights[span, :] = raised
        tops[index] = top
        sums[index] = jnp.sum(raised, axis=0, keepdims=True)
        return carry

    lax.fori_loop(0, chunks, score, 0)
    highest = jnp.max(tops[...], axis=0)
    shares = jnp.exp2((tops[...] - highest[None]) * log2_scale)
    total = jnp.sum(shares * sums[...], axis=0)
    sums[...] = shares / total[None]
    query_grad[...] = jnp.zeros_like(query_grad)

    def grads(index, carry):
        span = pl.ds(pl.multiple_of(index * CHUNK, CHUNK), CHUNK)
        probs = weights[span, :] * sums[index]
        score_grad = (probs * (prob_grad[span, :] - delta[...]) * scale).astype(BF16)
        probs_low = probs.astype(BF16)
        latent_part[span, :] = (dot(score_grad, absorbed[...]) + dot(probs_low, grad_out[...])).astype(BF16)
        query_grad[...] += dot_tn(keys[span, :], score_grad)
        return carry

    lax.fori_loop(0, chunks, grads, 0)
    for h in range(heads):
        cols = slice(h * NOPE, (h + 1) * NOPE)
        span = slice(h * TOK, (h + 1) * TOK)
        absorbed_grad = query_grad[:LATENT, span].astype(BF16)
        weight_part[:LATENT, cols] = dot(absorbed_grad, query_nope[:, cols]).astype(BF16)
        grad_nope[:, cols] = dot_tn(absorbed_grad, key_weight[:, cols]).astype(BF16)
    rope_grad = jnp.concatenate(
        [query_grad[LATENT : LATENT + ROPE, h * TOK : (h + 1) * TOK] for h in range(heads)], axis=0
    )
    grad_rope[...] = rope_grad.T.astype(BF16)


def attention(owner, keys, query_nope, query_rope, key_weight, value_weight, saved, output_grad):
    total = keys.shape[0]
    heads = query_nope.shape[1] // NOPE
    rows = heads * TOK
    chunks = total // CHUNK
    vmem = pl.BlockSpec(memory_space=pltpu.VMEM)
    return pl.pallas_call(
        attention_kernel,
        out_shape=(
            jax.ShapeDtypeStruct(query_nope.shape, BF16),
            jax.ShapeDtypeStruct(query_rope.shape, BF16),
            jax.ShapeDtypeStruct((total, LATENT), BF16),
            jax.ShapeDtypeStruct((2 * LATENT, query_nope.shape[1]), BF16),
        ),
        in_specs=[pl.BlockSpec(memory_space=pltpu.SMEM)] + [vmem] * 7,
        out_specs=(vmem,) * 4,
        scratch_shapes=[
            pltpu.VMEM((WIDE, rows), BF16),
            pltpu.VMEM((rows, LATENT), BF16),
            pltpu.VMEM((LATENT, rows), BF16),
            pltpu.VMEM((rows, LATENT), BF16),
            pltpu.VMEM((1, rows), F32),
            pltpu.VMEM((total, rows), F32),
            pltpu.VMEM((total, rows), F32),
            pltpu.VMEM((chunks, 1, rows), F32),
            pltpu.VMEM((chunks, 1, rows), F32),
            pltpu.VMEM((WIDE, rows), F32),
        ],
        compiler_params=pltpu.CompilerParams(vmem_limit_bytes=VMEM_LIMIT),
        name="attention_grads",
    )(owner, keys, query_nope, query_rope, key_weight, value_weight, saved, output_grad)


def reduce_kernel(
    latent,
    weight,
    out_latent,
    out_key,
    out_value,
    core_buf,
    z_buf,
    y_buf,
    x_buf,
    w_buf,
    w_near,
    w_all,
    core_send,
    core_recv,
    z_send,
    z_recv,
    y_send,
    y_recv,
    x_send,
    x_recv,
    last_send,
    last_recv,
    w_send,
    w_recv,
    wn_send,
    wn_recv,
    wb_send,
    wb_recv,
    wg_send,
    wg_recv,
):
    y, zh, zl, x, core = place()
    turn = 1 - 2 * core
    z = 2 * zh + zl
    sibling = device(y, zh, zl, x, 1 - core)
    y_peers = [device(wrap(y + d, NY), zh, zl, x, core) for d in range(1, NY)]
    zh_peers = [device(y, wrap(zh + d, NZH), zl, x, core) for d in range(1, NZH)]
    x_peers = [device(y, zh, zl, wrap(x + d, NX), core) for d in range(1, NX)]
    across = [device(y, zh, 1 - zl, x, core), device(y, zh, 1 - zl, x, 1 - core)]

    def z_device(where):
        return device(y, where // 2, lax.rem(where, 2), x, core)

    ring_far = z_device(wrap(z - 1 + 2 * zl, NZ))
    y_next = device(wrap(y + turn, NY), zh, zl, x, core)
    z_next = z_device(wrap(z + turn, NZ))
    greet([sibling] + y_peers + zh_peers + x_peers + across + [ring_far])

    core_copies = []
    for step in range(NZ):
        where = wrap(z + turn * (step + 1), NZ)
        core_copies.append(
            copy_to(
                latent.at[:, where // 2, 1 - core, lax.rem(where, 2)],
                core_buf.at[step],
                core_send.at[step],
                core_recv.at[step],
                sibling,
            )
        )
        core_copies[-1].start()

    half_y = NY // 2

    def z_copy(step, sub):
        part = pl.ds(sub * half_y, half_y)
        return copy_to(
            core_buf.at[step, part], z_buf.at[step, part], z_send.at[step, sub], z_recv.at[step, sub], z_next
        )

    def latent_step(step, sub):
        part = pl.ds(sub * half_y, half_y)
        if sub == 0:
            core_copies[step].wait_recv()
        where = wrap(z - turn * (step + 1), NZ)
        if step > 0:
            z_copy(step - 1, sub).wait_recv()
        own = latent.at[:, where // 2, core, lax.rem(where, 2)]

        def add(index, carry):
            row = sub * half_y + index
            value = own[row].astype(F32) + core_buf[step, row].astype(F32)
            if step > 0:
                value += z_buf[step - 1, row].astype(F32)
            core_buf[step, row] = value.astype(BF16)
            return carry

        lax.fori_loop(0, half_y, add, 0)
        if step < NZ - 1:
            z_copy(step, sub).start()

    half_z = NZH // 2

    def w_copy(step, sub):
        part = pl.ds(sub * half_z, half_z)
        if step == 0:
            source = weight.at[wrap(y - turn, NY), part]
        else:
            source = w_buf.at[step - 1, part]
        return copy_to(source, w_buf.at[step, part], w_send.at[step, sub], w_recv.at[step, sub], y_next)

    def weight_start():
        for sub in range(2):
            w_copy(0, sub).start()

    def weight_step(step, sub):
        where = wrap(y - turn * (step + 2), NY)
        w_copy(step, sub).wait_recv()

        def add(index, carry):
            row = sub * half_z + index
            value = w_buf[step, row].astype(F32) + weight[where, row].astype(F32)
            w_buf[step, row] = value.astype(BF16)
            return carry

        lax.fori_loop(0, half_z, add, 0)
        if step + 1 < NY - 1:
            w_copy(step + 1, sub).start()

    def near_copy(d):
        target = wrap(zh + d, NZH)
        return copy_to(
            w_buf.at[NY - 2, target], w_near.at[d - 1], wn_send.at[d - 1], wn_recv.at[d - 1], zh_peers[d - 1]
        )

    def weight_near():
        for d in range(1, NZH):
            near_copy(d).start()

    def back_copy(d, source):
        region = w_all.at[y, source]
        return copy_to(region, region, wb_send.at[d - 1], wb_recv.at[d - 1], zh_peers[d - 1])

    def weight_sum():
        value = w_buf[NY - 2, zh].astype(F32)
        for d in range(1, NZH):
            near_copy(d).wait_recv()
            value += w_near[d - 1].astype(F32)
        w_all[y, zh] = value.astype(BF16)
        for d in range(1, NZH):
            back_copy(d, zh).start()

    def weight_collect():
        for d in range(1, NZH):
            back_copy(d, wrap(zh - d, NZH)).wait_recv()

    def spread_copy(step, sub, where):
        region = w_all.at[where, pl.ds(sub * half_z, half_z)]
        return copy_to(region, region, wg_send.at[step, sub], wg_recv.at[step, sub], y_next)

    def spread_start(step, sub):
        spread_copy(step, sub, wrap(y - turn * step, NY)).start()

    def spread_step(step, sub):
        spread_copy(step, sub, wrap(y - turn * (step + 1), NY)).wait_recv()
        if step + 1 < NY - 1:
            spread_start(step + 1, sub)

    weight_jobs = [weight_start]
    for step in range(NY - 1):
        for sub in range(2):
            weight_jobs.append(functools.partial(weight_step, step, sub))
    weight_jobs += [weight_near, weight_sum, weight_collect]
    weight_jobs.append(lambda: [spread_start(0, sub) for sub in range(2)])
    for step in range(NY - 1):
        for sub in range(2):
            weight_jobs.append(functools.partial(spread_step, step, sub))
    latent_jobs = []
    for step in range(NZ):
        for sub in range(2):
            latent_jobs.append(functools.partial(latent_step, step, sub))

    def y_copy(d):
        target = wrap(y + d, NY)
        return copy_to(
            core_buf.at[NZ - 1, target], y_buf.at[d - 1], y_send.at[d - 1], y_recv.at[d - 1], y_peers[d - 1]
        )

    def latent_y_start():
        for d in range(1, NY):
            y_copy(d).start()

    def x_copy(d, source):
        return copy_to(
            x_buf.at[source], x_buf.at[source], x_send.at[d - 1], x_recv.at[d - 1], x_peers[d - 1]
        )

    def latent_y_sum():
        value = core_buf[NZ - 1, y].astype(F32)
        for d in range(1, NY):
            y_copy(d).wait_recv()
            value += y_buf[d - 1].astype(F32)
        x_buf[x] = value.astype(BF16)
        for d in range(1, NX):
            x_copy(d, x).start()

    last_peers = [sibling] + across

    def last_copy(index, half, low):
        region = out_latent.at[half, low]
        return copy_to(region, region, last_send.at[index], last_recv.at[index], last_peers[index])

    def latent_x_sum():
        for d in range(1, NX):
            x_copy(d, wrap(x - d, NX)).wait_recv()
        value = x_buf[0].astype(F32)
        for index in range(1, NX):
            value += x_buf[index].astype(F32)
        out_latent[core, zl] = value.astype(BF16)
        for index in range(3):
            last_copy(index, core, zl).start()

    def latent_last():
        last_copy(0, 1 - core, zl).wait_recv()
        last_copy(1, core, 1 - zl).wait_recv()
        last_copy(2, 1 - core, 1 - zl).wait_recv()

    latent_jobs += [latent_y_start, latent_y_sum, latent_x_sum]

    done = 0
    for index, job in enumerate(weight_jobs):
        job()
        upto = (index + 1) * len(latent_jobs) // len(weight_jobs)
        while done < upto:
            latent_jobs[done]()
            done += 1

    for k in range(NY // 2):
        out_key[k] = w_all[k].astype(F32)
        out_value[k] = w_all[NY // 2 + k].astype(F32)
    latent_last()

    for copy in core_copies:
        copy.wait_send()
    for step in range(NZ - 1):
        for sub in range(2):
            z_copy(step, sub).wait_send()
    for step in range(NY - 1):
        for sub in range(2):
            w_copy(step, sub).wait_send()
            spread_copy(step, sub, wrap(y - turn * step, NY)).wait_send()
    for d in range(1, NY):
        y_copy(d).wait_send()
    for d in range(1, NX):
        x_copy(d, x).wait_send()
    for d in range(1, NZH):
        near_copy(d).wait_send()
        back_copy(d, zh).wait_send()
    for index in range(3):
        last_copy(index, core, zl).wait_send()


def reduce_grads(latent_part, weight_part):
    latent = latent_part.reshape(NY, NZH, 2, 2, 32, LATENT)
    wide = weight_part.shape[1]
    piece = 2 * LATENT // (NY * NZH)
    weight = weight_part.reshape(NY, NZH, piece, wide)
    vmem = pl.BlockSpec(memory_space=pltpu.VMEM)
    dma = pltpu.SemaphoreType.DMA
    pairs = lambda *shape: [dma(shape), dma(shape)]
    out = pl.pallas_call(
        reduce_kernel,
        out_shape=(
            jax.ShapeDtypeStruct((2, 2, 32, LATENT), BF16),
            jax.ShapeDtypeStruct((NY // 2, NZH, piece, wide), F32),
            jax.ShapeDtypeStruct((NY // 2, NZH, piece, wide), F32),
        ),
        in_specs=[vmem, vmem],
        out_specs=(vmem,) * 3,
        scratch_shapes=[
            pltpu.VMEM((NZ, NY, 32, LATENT), BF16),
            pltpu.VMEM((NZ - 1, NY, 32, LATENT), BF16),
            pltpu.VMEM((NY - 1, 32, LATENT), BF16),
            pltpu.VMEM((NX, 32, LATENT), BF16),
            pltpu.VMEM((NY - 1, NZH, piece, wide), BF16),
            pltpu.VMEM((NZH - 1, piece, wide), BF16),
            pltpu.VMEM((NY, NZH, piece, wide), BF16),
        ]
        + pairs(NZ)
        + pairs(NZ - 1, 2)
        + pairs(NY - 1)
        + pairs(NX - 1)
        + pairs(3)
        + pairs(NY - 1, 2)
        + pairs(NZH - 1)
        + pairs(NZH - 1)
        + pairs(NY - 1, 2),
        compiler_params=pltpu.CompilerParams(
            collective_id=1, has_side_effects=True, vmem_limit_bytes=VMEM_LIMIT
        ),
        name="reduce_grads",
    )(latent, weight)
    return (
        out[0].reshape(4 * 32, LATENT),
        out[1].reshape(LATENT, wide),
        out[2].reshape(LATENT, wide),
    )


def on_device(
    block_owner,
    query_nope,
    query_rope,
    latent_cache,
    key_up_weight,
    value_up_weight,
    saved_output,
    output_grad,
):
    keys = gather_keys(block_owner, latent_cache).reshape(NY * NZH * TOK, WIDE)
    grad_nope, grad_rope, latent_part, weight_part = attention(
        block_owner, keys, query_nope, query_rope, key_up_weight, value_up_weight, saved_output, output_grad
    )
    grad_latent, grad_key, grad_value = reduce_grads(latent_part, weight_part)
    return grad_nope, grad_rope, grad_latent, grad_key, grad_value


def solution(mesh):
    return jax.shard_map(
        on_device,
        mesh=mesh,
        in_specs=(
            P("ctx"),
            P("ctx", "head"),
            P("ctx", "head"),
            P("ctx", None),
            P(None, "head"),
            P(None, "head"),
            P("ctx", "head"),
            P("ctx", "head"),
        ),
        out_specs=(
            P("ctx", "head"),
            P("ctx", "head"),
            P("ctx", None),
            P(None, "head"),
            P(None, "head"),
        ),
        check_vma=False,
    )
```

```python
import math

import jax
import jax.numpy as jnp
from jax import lax
from jax.experimental import pallas as pl
from jax.experimental.pallas import tpu as pltpu
from jax.sharding import PartitionSpec as P

LATENT = 512
ROPE = 64
NOPE = 128
NY, NZH, NX = 8, 4, 4
NZ = 2 * NZH
BLOCKS = 64
WIDE = LATENT + ROPE + BLOCKS
TOK = 128
GROUPS = 4
HIDDEN = -1e30
BF16 = jnp.bfloat16
F32 = jnp.float32
VMEM_LIMIT = 60 * 1024 * 1024


def device(y, zh, zl, x, core):
    return (y * NZH + zh, zl * (2 * NX) + x * 2 + core)


def copy_to(src, dst, send_sem, recv_sem, target):
    return pltpu.make_async_remote_copy(
        src_ref=src,
        dst_ref=dst,
        send_sem=send_sem,
        recv_sem=recv_sem,
        device_id=target,
        device_id_type=pl.DeviceIdType.MESH,
    )


def wrap(index, size):
    return lax.rem(index + 2 * size, size)


def each(start, stop, body):
    def step(index, carry):
        body(index)
        return carry

    lax.fori_loop(start, stop, step, 0)


def rows(start, size, step=16):
    return pl.ds(pl.multiple_of(start, step), size)


def dot(left, right):
    return jnp.dot(left, right, preferred_element_type=F32)


def dot_nt(left, right):
    return lax.dot_general(left, right, (((1,), (1,)), ((), ())), preferred_element_type=F32)


def dot_tn(left, right):
    return lax.dot_general(left, right, (((0,), (0,)), ((), ())), preferred_element_type=F32)


def fused_kernel(
    owner,
    latent,
    query_nope,
    query_rope,
    key_weight,
    value_weight,
    saved,
    output_grad,
    grad_nope,
    grad_rope,
    weight_all,
    latent_out,
    keys,
    query_t,
    absorbed,
    grad_out_t,
    grad_out,
    delta,
    weights,
    prob_grad,
    score_low,
    probs_low,
    tops,
    sums,
    query_grad,
    weight_part,
    wa_in,
    wb_in,
    wa_sum,
    wb_sum,
    wa_near,
    wb_near,
    part,
    pair,
    ring,
    mine,
    y_in,
    z_in,
    y_sum,
    z_sum,
    y_last,
    z_last,
    near_y_send,
    near_y_recv,
    near_z_send,
    near_z_recv,
    ring_send,
    ring_recv,
    pass_send,
    pass_recv,
    wy_send,
    wy_recv,
    wz_send,
    wz_recv,
    pair_send,
    pair_recv,
    x_send,
    x_recv,
    ly_send,
    ly_recv,
    lz_send,
    lz_recv,
    head_send,
    head_recv,
):
    heads = query_nope.shape[1] // NOPE
    count = heads * TOK
    scale = (NOPE + ROPE) ** -0.5
    log2_scale = scale * math.log2(math.e)
    half = keys.shape[1] // 2
    chunks = keys.shape[0]

    ctx, head = lax.axis_index("ctx"), lax.axis_index("head")
    y, zh = ctx // NZH, lax.rem(ctx, NZH)
    zl = head // (2 * NX)
    x = lax.rem(head // 2, NX)
    core = lax.rem(head, 2)
    z = 2 * zh + zl
    turn = 1 - 2 * core
    sibling = device(y, zh, zl, x, 1 - core)
    heads_all = 4 * NX

    def y_peer(where):
        return device(where, zh, zl, x, core)

    def z_peer(where):
        return device(y, where // 2, lax.rem(where, 2), x, core)

    def zh_peer(where):
        return device(y, where, zl, x, core)

    def x_peer(where):
        return device(y, zh, zl, where, core)

    column = lax.broadcasted_iota(jnp.int32, (16, BLOCKS), 1)
    for side in range(2):
        mark = jnp.where(column == owner[side], 1.0, 0.0).astype(BF16)
        for piece in range(4):
            start = side * 64 + piece * 16
            if piece < 2:
                where, spot = y, rows(side * half + zh * 32 + piece * 16, 16)
            else:
                where, spot = NY + 2 * zh + piece - 2, rows(side * half + y * 16, 16)
            keys[where, spot, : LATENT + ROPE] = latent[start : start + 16, :]
            keys[where, spot, LATENT + ROPE :] = mark

    barrier = pltpu.get_barrier_semaphore()

    def hail(target):
        pl.semaphore_signal(barrier, inc=1, device_id=target, device_id_type=pl.DeviceIdType.MESH)

    each(1, NY, lambda d: hail(y_peer(wrap(y + d, NY))))
    each(1, NZ, lambda d: hail(z_peer(wrap(z + d, NZ))))
    each(1, heads_all, lambda d: hail((ctx, wrap(head + d, heads_all))))
    pl.semaphore_wait(barrier, NY - 1 + NZ - 1 + heads_all - 1)

    def near_y(d, spot):
        region = keys.at[NY + z, rows(core * half + spot * 16, 16)]
        return copy_to(region, region, near_y_send.at[d - 1], near_y_recv.at[d - 1], y_peer(wrap(y + d, NY)))

    def near_z(d, spot):
        region = keys.at[y, rows(core * half + spot * 32, 32, 32)]
        return copy_to(region, region, near_z_send.at[d - 1], near_z_recv.at[d - 1], zh_peer(wrap(zh + d, NZH)))

    each(1, NZH, lambda d: near_z(d, zh).start())
    each(1, NY, lambda d: near_y(d, y).start())

    rope_t = query_rope[...].astype(F32).T.astype(BF16)
    block = lax.broadcasted_iota(jnp.int32, (BLOCKS, TOK), 0)
    token = lax.broadcasted_iota(jnp.int32, (BLOCKS, TOK), 1)
    limit = jnp.where(token < TOK // 2, owner[0], owner[1])
    bias = jnp.where(block <= limit, 0.0, HIDDEN).astype(BF16)
    for h in range(heads):
        cols = slice(h * NOPE, (h + 1) * NOPE)
        span = slice(h * TOK, (h + 1) * TOK)
        query, weight = query_nope[:, cols], key_weight[:, cols]
        query_t[:LATENT, span] = dot_nt(weight, query).astype(BF16)
        query_t[LATENT : LATENT + ROPE, span] = rope_t[h * ROPE : (h + 1) * ROPE, :]
        query_t[LATENT + ROPE :, span] = bias
        grad_out_t[:, span] = dot_nt(value_weight[:, cols], output_grad[:, cols]).astype(BF16)

    places = ((y, NY, 0), (z, NZ, NY))

    def ring_target(axis, rel):
        way = turn if rel == 0 else -turn
        return y_peer(wrap(y + way, NY)) if axis == 0 else z_peer(wrap(z + way, NZ))

    def ring_chunk(axis, rel, step):
        at, size, base = places[axis]
        way = turn if rel == 0 else -turn
        return base + wrap(at - way * step, size)

    def ring_copy(axis, rel, step, where):
        region = keys.at[where, rows(core * half, half, half)]
        return copy_to(
            region, region, ring_send.at[axis, rel, step], ring_recv.at[axis, rel, step], ring_target(axis, rel)
        )

    def pass_copy(axis, slot, where, side):
        region = keys.at[where, rows(side * half, half, half)]
        return copy_to(region, region, pass_send.at[axis, slot], pass_recv.at[axis, slot], sibling)

    def score(where):
        rows_in = keys[where]
        weights[where] = dot(rows_in, query_t[...])
        prob_grad[where] = dot(rows_in[:, :LATENT], grad_out_t[...])

        def hide(first, size, offset):
            for side in range(2):
                spot = rows(side * half + first, size)
                key_row = lax.broadcasted_iota(jnp.int32, (size, count), 0) + offset
                query_row = lax.rem(lax.broadcasted_iota(jnp.int32, (size, count), 1), TOK) - side * 64
                later = (query_row >= 0) & (query_row < 64) & (key_row > query_row)
                weights[where, spot, :] = jnp.where(later, HIDDEN, weights[where, spot, :])

        @pl.when(where == y)
        def _():
            hide(zh * 32, 32, 0)

        low = where - NY - 2 * zh

        @pl.when((low >= 0) & (low < 2))
        def _():
            hide(y * 16, 16, 32 + low * 16)

        raw = weights[where]
        top = jnp.max(raw, axis=0, keepdims=True)
        raised = jnp.exp2((raw - top) * log2_scale)
        weights[where] = raised
        tops[where] = top
        sums[where] = jnp.sum(raised, axis=0, keepdims=True)

    each(1, NZH, lambda d: near_z(d, wrap(zh - d, NZH)).wait_recv())
    for rel in range(2):
        if rel == 0 or NY > 2:
            ring_copy(0, rel, 0, y).start()
    each(1, NY, lambda d: near_y(d, wrap(y - d, NY)).wait_recv())
    for rel in range(2):
        if rel == 0 or NZ > 2:
            ring_copy(1, rel, 0, NY + z).start()
    pass_copy(0, 0, y, core).start()
    pass_copy(1, 0, NY + z, core).start()

    for h in range(heads):
        cols = slice(h * NOPE, (h + 1) * NOPE)
        span = slice(h * TOK, (h + 1) * TOK)
        side, at = h // (heads // 2), h % (heads // 2)
        place = slice(at * NOPE, (at + 1) * NOPE)
        out = output_grad[:, cols]
        grads = dot_nt(out, value_weight[:, cols]).astype(BF16)
        grad_out[span, :] = grads
        held = saved[:, h * LATENT : (h + 1) * LATENT]
        product = grads.astype(F32) * held.astype(F32)
        delta[:, span] = jnp.sum(product.T, axis=0, keepdims=True)
        weight_part[0, side, :, place] = dot_tn(held, out).astype(BF16)
        absorbed[span, :] = dot_nt(query_nope[:, cols], key_weight[:, cols]).astype(BF16)

    pass_copy(0, 0, y, 1 - core).wait_recv()
    pass_copy(1, 0, NY + z, 1 - core).wait_recv()
    each(0, 2, lambda i: score(i * (NY + z) + (1 - i) * y))

    ra, rb, rp = LATENT // NY, LATENT // NZH, LATENT // (NY * NZH)

    def wy_copy(w, stage, d, src, dst):
        return copy_to(
            src, dst, wy_send.at[w, stage, d - 1], wy_recv.at[w, stage, d - 1], y_peer(wrap(y + d, NY))
        )

    def wz_copy(w, stage, d, src, dst):
        return copy_to(
            src, dst, wz_send.at[w, stage, d - 1], wz_recv.at[w, stage, d - 1], zh_peer(wrap(zh + d, NZH))
        )

    def a_first(w, d):
        return wy_copy(w, 0, d, weight_part.at[w, 0, rows(wrap(y + d, NY) * ra, ra)], wa_in.at[w, d - 1])

    def b_first(w, d):
        return wz_copy(w, 0, d, weight_part.at[w, 1, rows(wrap(zh + d, NZH) * rb, rb)], wb_in.at[w, d - 1])

    def a_second(w, d):
        return wz_copy(w, 1, d, wa_sum.at[w, rows(wrap(zh + d, NZH) * rp, rp)], wa_near.at[w, d - 1])

    def b_second(w, d):
        return wy_copy(w, 1, d, wb_sum.at[w, rows(wrap(y + d, NY) * rp, rp)], wb_near.at[w, d - 1])

    def a_third(w, d, where):
        region = weight_all.at[w, 0, rows(y * ra + where * rp, rp)]
        return wz_copy(w, 2, d, region, region)

    def b_third(w, d, where):
        region = weight_all.at[w, 1, rows(zh * rb + where * rp, rp)]
        return wy_copy(w, 2, d, region, region)

    def a_fourth(w, d, where):
        region = weight_all.at[w, 0, rows(where * ra, ra)]
        return wy_copy(w, 3, d, region, region)

    def b_fourth(w, d, where):
        region = weight_all.at[w, 1, rows(where * rb, rb)]
        return wz_copy(w, 3, d, region, region)

    def weight_first(w):
        each(1, NY, lambda d: a_first(w, d).start())
        each(1, NZH, lambda d: b_first(w, d).start())

    def weight_second(w):
        each(1, NY, lambda d: a_first(w, d).wait_recv())
        total = weight_part[w, 0, rows(y * ra, ra), :].astype(F32)
        for d in range(1, NY):
            total += wa_in[w, d - 1].astype(F32)
        wa_sum[w] = total.astype(BF16)
        each(1, NZH, lambda d: a_second(w, d).start())
        each(1, NZH, lambda d: b_first(w, d).wait_recv())
        total = weight_part[w, 1, rows(zh * rb, rb), :].astype(F32)
        for d in range(1, NZH):
            total += wb_in[w, d - 1].astype(F32)
        wb_sum[w] = total.astype(BF16)
        each(1, NY, lambda d: b_second(w, d).start())

    def weight_third(w):
        each(1, NZH, lambda d: a_second(w, d).wait_recv())
        total = wa_sum[w, rows(zh * rp, rp), :].astype(F32)
        for d in range(1, NZH):
            total += wa_near[w, d - 1].astype(F32)
        weight_all[w, 0, rows(y * ra + zh * rp, rp), :] = total.astype(BF16)
        each(1, NZH, lambda d: a_third(w, d, zh).start())
        each(1, NY, lambda d: b_second(w, d).wait_recv())
        total = wb_sum[w, rows(y * rp, rp), :].astype(F32)
        for d in range(1, NY):
            total += wb_near[w, d - 1].astype(F32)
        weight_all[w, 1, rows(zh * rb + y * rp, rp), :] = total.astype(BF16)
        each(1, NY, lambda d: b_third(w, d, y).start())

    def weight_fourth(w):
        each(1, NZH, lambda d: a_third(w, d, wrap(zh - d, NZH)).wait_recv())
        each(1, NY, lambda d: a_fourth(w, d, y).start())
        each(1, NY, lambda d: b_third(w, d, wrap(y - d, NY)).wait_recv())
        each(1, NZH, lambda d: b_fourth(w, d, zh).start())

    def weight_last(w):
        each(1, NY, lambda d: a_fourth(w, d, wrap(y - d, NY)).wait_recv())
        each(1, NZH, lambda d: b_fourth(w, d, wrap(zh - d, NZH)).wait_recv())

    def weight_sent(w):
        def over_y(d):
            a_first(w, d).wait_send()
            b_second(w, d).wait_send()
            b_third(w, d, y).wait_send()
            a_fourth(w, d, y).wait_send()

        def over_z(d):
            b_first(w, d).wait_send()
            a_second(w, d).wait_send()
            a_third(w, d, zh).wait_send()
            b_fourth(w, d, zh).wait_send()

        each(1, NY, over_y)
        each(1, NZH, over_z)

    last = NY // 2 - 1
    for step in range(last):
        for rel in range(2):
            for axis in range(2):
                where = ring_chunk(axis, rel, step + 1)
                ring_copy(axis, rel, step, where).wait_recv()
                if rel == 0 or step + 1 < last:
                    ring_copy(axis, rel, step + 1, where).start()
                pass_copy(axis, 1 + 2 * step + rel, where, core).start()
        for rel in range(2):
            for axis in range(2):
                where = ring_chunk(axis, 1 - rel, step + 1)
                pass_copy(axis, 1 + 2 * step + rel, where, 1 - core).wait_recv()

        def arrived(i):
            axis, sign = i // 2, 1 - 2 * lax.rem(i, 2)
            score((1 - axis) * wrap(y - sign * (step + 1), NY) + axis * (NY + wrap(z - sign * (step + 1), NZ)))

        each(0, 4, arrived)
    for axis in range(2):
        where = ring_chunk(axis, 0, last + 1)
        ring_copy(axis, 0, last, where).wait_recv()
        pass_copy(axis, 1 + 2 * last, where, core).start()
    weight_first(0)
    for axis in range(2):
        pass_copy(axis, 1 + 2 * last, ring_chunk(axis, 0, last + 1), 1 - core).wait_recv()
    each(0, 2, lambda i: score((1 - i) * wrap(y + last + 1, NY) + i * (NY + wrap(z + last + 1, NZ))))

    highest = jnp.max(tops[...], axis=0)
    shares = jnp.exp2((tops[...] - highest[None]) * log2_scale)
    total = jnp.sum(shares * sums[...], axis=0)
    sums[...] = shares / total[None]
    query_grad[...] = jnp.zeros_like(query_grad)

    def gradients(where):
        probs = weights[where] * sums[where]
        grads = (probs * (prob_grad[where] - delta[...]) * scale).astype(BF16)
        score_low[where] = grads
        probs_low[where] = probs.astype(BF16)
        query_grad[...] += dot_tn(keys[where], grads)

    each(0, chunks // 2, gradients)
    weight_second(0)
    each(chunks // 2, chunks, gradients)
    weight_third(0)
    for h in range(heads):
        cols = slice(h * NOPE, (h + 1) * NOPE)
        span = slice(h * TOK, (h + 1) * TOK)
        side, at = h // (heads // 2), h % (heads // 2)
        place = slice(at * NOPE, (at + 1) * NOPE)
        weight_part[1, side, :, place] = dot(query_grad[:LATENT, span].astype(BF16), query_nope[:, cols]).astype(BF16)
    weight_first(1)

    wide = LATENT // NX
    size = chunks // GROUPS
    x_next, x_back = x_peer(wrap(x + turn, NX)), x_peer(wrap(x - turn, NX))

    def pair_copy(g):
        group = pl.ds(g * size, size)
        return copy_to(
            part.at[:, group, rows((1 - core) * half, half, half)],
            pair.at[:, group],
            pair_send.at[g],
            pair_recv.at[g],
            sibling,
        )

    def x_copy(kind, g):
        group = pl.ds(g * size, size)
        target = x_back if kind == 1 else x_next
        where = wrap(x + 2, NX) if kind == 0 else wrap(x - turn, NX) if kind == 1 else wrap(x + turn, NX)
        return copy_to(
            pair.at[where, group], ring.at[kind, group], x_send.at[kind, g], x_recv.at[kind, g], target
        )

    def terms(g):
        def one(i):
            where = g * size + i
            value = dot(score_low[where], absorbed[...]) + dot(probs_low[where], grad_out[...])
            for k in range(NX):
                part[k, where] = value[:, k * wide : (k + 1) * wide].astype(BF16)

        each(0, size, one)
        pair_copy(g).start()

    def pair_sum(g):
        pair_copy(g).wait_recv()

        def one(i):
            where = g * size + i
            for k in range(NX):
                value = part[k, where, rows(core * half, half, half), :].astype(F32) + pair[k, where].astype(F32)
                pair[k, where] = value.astype(BF16)

        each(0, size, one)
        x_copy(0, g).start()
        x_copy(1, g).start()

    def x_sum(g):
        x_copy(0, g).wait_recv()
        to = wrap(x + turn, NX)

        def one(i):
            where = g * size + i
            pair[to, where] = (pair[to, where].astype(F32) + ring[0, where].astype(F32)).astype(BF16)

        each(0, size, one)
        x_copy(2, g).start()

    def x_last(g):
        x_copy(1, g).wait_recv()
        x_copy(2, g).wait_recv()

        def one(i):
            where = g * size + i
            value = pair[x, where].astype(F32) + ring[1, where].astype(F32) + ring[2, where].astype(F32)
            mine[where] = value.astype(BF16)

        each(0, size, one)

    terms(0)
    weight_fourth(0)
    terms(1)
    pair_sum(0)
    weight_second(1)
    terms(2)
    pair_sum(1)
    x_sum(0)
    terms(3)
    pair_sum(2)
    weight_third(1)
    x_sum(1)
    x_last(0)
    pair_sum(3)
    weight_fourth(1)
    x_sum(2)
    x_last(1)
    for h in range(heads):
        cols = slice(h * NOPE, (h + 1) * NOPE)
        span = slice(h * TOK, (h + 1) * TOK)
        grad_nope[:, cols] = dot_tn(query_grad[:LATENT, span].astype(BF16), key_weight[:, cols]).astype(BF16)
    x_sum(3)
    x_last(2)
    rope_grad = jnp.concatenate(
        [query_grad[LATENT : LATENT + ROPE, h * TOK : (h + 1) * TOK] for h in range(heads)], axis=0
    )
    grad_rope[...] = rope_grad.T.astype(BF16)
    x_last(3)

    def ly_copy(stage, d, src, dst):
        return copy_to(src, dst, ly_send.at[stage, d - 1], ly_recv.at[stage, d - 1], y_peer(wrap(y + d, NY)))

    def lz_copy(stage, d, src, dst):
        return copy_to(src, dst, lz_send.at[stage, d - 1], lz_recv.at[stage, d - 1], z_peer(wrap(z + d, NZ)))

    def y_first(d):
        return ly_copy(0, d, mine.at[wrap(y + d, NY)], y_in.at[d - 1])

    def z_first(d):
        return lz_copy(0, d, mine.at[NY + wrap(z + d, NZ)], z_in.at[d - 1])

    def y_second(d):
        return ly_copy(1, d, z_sum.at[rows(wrap(y + d, NY) * 16, 16)], y_last.at[d - 1])

    def z_second(d):
        return lz_copy(1, d, y_sum.at[rows(wrap(z + d, NZ) * 16, 16)], z_last.at[d - 1])

    each(1, NY, lambda d: y_first(d).start())
    each(1, NZ, lambda d: z_first(d).start())
    weight_last(0)
    each(1, NY, lambda d: y_first(d).wait_recv())
    total = mine[y].astype(F32)
    for d in range(1, NY):
        total += y_in[d - 1].astype(F32)
    y_sum[...] = total.astype(BF16)
    each(1, NZ, lambda d: z_second(d).start())
    each(1, NZ, lambda d: z_first(d).wait_recv())
    total = mine[NY + z].astype(F32)
    for d in range(1, NZ):
        total += z_in[d - 1].astype(F32)
    z_sum[...] = total.astype(BF16)
    each(1, NY, lambda d: y_second(d).start())

    def head_copy(d, who):
        region = latent_out.at[lax.rem(who, 2), who // (2 * NX), lax.rem(who // 2, NX)]
        return copy_to(
            region, region, head_send.at[d - 1], head_recv.at[d - 1], (ctx, wrap(head + d, heads_all))
        )

    each(1, NZ, lambda d: z_second(d).wait_recv())
    total = y_sum[rows(z * 16, 16), :].astype(F32)
    for d in range(1, NZ):
        total += z_last[d - 1].astype(F32)
    latent_out[core, zl, x, 0] = total.astype(BF16)
    each(1, NY, lambda d: y_second(d).wait_recv())
    total = z_sum[rows(y * 16, 16), :].astype(F32)
    for d in range(1, NY):
        total += y_last[d - 1].astype(F32)
    latent_out[core, zl, x, 1] = total.astype(BF16)
    each(1, heads_all, lambda d: head_copy(d, head).start())

    weight_last(1)
    each(1, NZH, lambda d: near_z(d, zh).wait_send())
    each(1, NY, lambda d: near_y(d, y).wait_send())
    for axis in range(2):
        for rel in range(2):
            for step in range(last + 1 - rel):
                ring_copy(axis, rel, step, ring_chunk(axis, rel, step)).wait_send()
        pass_copy(axis, 0, y if axis == 0 else NY + z, core).wait_send()
        for step in range(last + 1):
            for rel in range(2 if step < last else 1):
                pass_copy(axis, 1 + 2 * step + rel, ring_chunk(axis, rel, step + 1), core).wait_send()
    weight_sent(0)
    weight_sent(1)
    for g in range(GROUPS):
        pair_copy(g).wait_send()
        for kind in range(3):
            x_copy(kind, g).wait_send()

    def sent_y(d):
        y_first(d).wait_send()
        y_second(d).wait_send()

    def sent_z(d):
        z_first(d).wait_send()
        z_second(d).wait_send()

    each(1, NY, sent_y)
    each(1, NZ, sent_z)
    each(1, heads_all, lambda d: head_copy(d, wrap(head - d, heads_all)).wait_recv())
    each(1, heads_all, lambda d: head_copy(d, head).wait_send())


def fused(owner, latent, query_nope, query_rope, key_weight, value_weight, saved, output_grad):
    heads = query_nope.shape[1] // NOPE
    count = heads * TOK
    half = NZH * 32
    chunks = NY + NZ
    wide = LATENT // NX
    cols = count // 2
    ra, rb, rp = LATENT // NY, LATENT // NZH, LATENT // (NY * NZH)
    vmem = pl.BlockSpec(memory_space=pltpu.VMEM)
    dma = pltpu.SemaphoreType.DMA
    hold = pltpu.VMEM

    def sems(*shape):
        return [dma(shape), dma(shape)]

    return pl.pallas_call(
        fused_kernel,
        out_shape=(
            jax.ShapeDtypeStruct(query_nope.shape, BF16),
            jax.ShapeDtypeStruct(query_rope.shape, BF16),
            jax.ShapeDtypeStruct((2, 2, LATENT, cols), BF16),
            jax.ShapeDtypeStruct((2, 2, NX, 2, 16, wide), BF16),
        ),
        in_specs=[pl.BlockSpec(memory_space=pltpu.SMEM)] + [vmem] * 7,
        out_specs=(vmem,) * 4,
        scratch_shapes=[
            hold((chunks, 2 * half, WIDE), BF16),
            hold((WIDE, count), BF16),
            hold((count, LATENT), BF16),
            hold((LATENT, count), BF16),
            hold((count, LATENT), BF16),
            hold((1, count), F32),
            hold((chunks, 2 * half, count), F32),
            hold((chunks, 2 * half, count), F32),
            hold((chunks, 2 * half, count), BF16),
            hold((chunks, 2 * half, count), BF16),
            hold((chunks, 1, count), F32),
            hold((chunks, 1, count), F32),
            hold((WIDE, count), F32),
            hold((2, 2, LATENT, cols), BF16),
            hold((2, NY - 1, ra, cols), BF16),
            hold((2, NZH - 1, rb, cols), BF16),
            hold((2, ra, cols), BF16),
            hold((2, rb, cols), BF16),
            hold((2, NZH - 1, rp, cols), BF16),
            hold((2, NY - 1, rp, cols), BF16),
            hold((NX, chunks, 2 * half, wide), BF16),
            hold((NX, chunks, half, wide), BF16),
            hold((3, chunks, half, wide), BF16),
            hold((chunks, half, wide), BF16),
            hold((NY - 1, half, wide), BF16),
            hold((NZ - 1, half, wide), BF16),
            hold((half, wide), BF16),
            hold((half, wide), BF16),
            hold((NY - 1, 16, wide), BF16),
            hold((NZ - 1, 16, wide), BF16),
        ]
        + sems(NY - 1)
        + sems(NZH - 1)
        + sems(2, 2, NY // 2)
        + sems(2, NY)
        + sems(2, 4, NY - 1)
        + sems(2, 4, NZH - 1)
        + sems(GROUPS)
        + sems(3, GROUPS)
        + sems(2, NY - 1)
        + sems(2, NZ - 1)
        + sems(4 * NX - 1),
        compiler_params=pltpu.CompilerParams(
            collective_id=0, has_side_effects=True, vmem_limit_bytes=VMEM_LIMIT
        ),
        name="fused_grads",
    )(owner, latent, query_nope, query_rope, key_weight, value_weight, saved, output_grad)


def finish_kernel(nope, rope, weight, latent, grad_nope, grad_rope, grad_latent, grad_key, grad_value):
    grad_nope[...] = nope[...]
    grad_rope[...] = rope[...]
    wide = LATENT // NX
    cols = weight.shape[3]
    for core in range(2):
        for low in range(2):
            for x in range(NX):
                for kind in range(2):
                    start = core * 64 + kind * 32 + low * 16
                    grad_latent[start : start + 16, x * wide : (x + 1) * wide] = latent[core, low, x, kind]
    for side in range(2):
        grad_value[:, side * cols : (side + 1) * cols] = weight[0, side].astype(F32)
        grad_key[:, side * cols : (side + 1) * cols] = weight[1, side].astype(F32)


def finish(nope, rope, weight, latent):
    vmem = pl.BlockSpec(memory_space=pltpu.VMEM)
    cols = 2 * weight.shape[3]
    return pl.pallas_call(
        finish_kernel,
        out_shape=(
            jax.ShapeDtypeStruct(nope.shape, BF16),
            jax.ShapeDtypeStruct(rope.shape, BF16),
            jax.ShapeDtypeStruct((TOK, LATENT), BF16),
            jax.ShapeDtypeStruct((LATENT, cols), F32),
            jax.ShapeDtypeStruct((LATENT, cols), F32),
        ),
        in_specs=[vmem] * 4,
        out_specs=(vmem,) * 5,
        compiler_params=pltpu.CompilerParams(vmem_limit_bytes=VMEM_LIMIT),
        name="finish",
    )(nope, rope, weight, latent)


def on_device(
    block_owner,
    query_nope,
    query_rope,
    latent_cache,
    key_up_weight,
    value_up_weight,
    saved_output,
    output_grad,
):
    return finish(
        *fused(
            block_owner,
            latent_cache,
            query_nope,
            query_rope,
            key_up_weight,
            value_up_weight,
            saved_output,
            output_grad,
        )
    )


def solution(mesh):
    return jax.shard_map(
        on_device,
        mesh=mesh,
        in_specs=(
            P("ctx"),
            P("ctx", "head"),
            P("ctx", "head"),
            P("ctx", None),
            P(None, "head"),
            P(None, "head"),
            P("ctx", "head"),
            P("ctx", "head"),
        ),
        out_specs=(
            P("ctx", "head"),
            P("ctx", "head"),
            P("ctx", None),
            P(None, "head"),
            P(None, "head"),
        ),
        check_vma=False,
    )
```

```python
import math

import jax
import jax.numpy as jnp
from jax import lax
from jax.experimental import pallas as pl
from jax.experimental.pallas import tpu as pltpu
from jax.sharding import PartitionSpec as P

LATENT = 512
ROPE = 64
NOPE = 128
NY, NZH, NX = 8, 4, 4
NZ = 2 * NZH
BLOCKS = 64
WIDE = LATENT + ROPE + BLOCKS
TOK = 128
GROUPS = 4
HIDDEN = -1e30
BF16 = jnp.bfloat16
F32 = jnp.float32
VMEM_LIMIT = 60 * 1024 * 1024


def device(y, zh, zl, x, core):
    return (y * NZH + zh, zl * (2 * NX) + x * 2 + core)


def copy_to(src, dst, send_sem, recv_sem, target):
    return pltpu.make_async_remote_copy(
        src_ref=src,
        dst_ref=dst,
        send_sem=send_sem,
        recv_sem=recv_sem,
        device_id=target,
        device_id_type=pl.DeviceIdType.MESH,
    )


def wrap(index, size):
    return lax.rem(index + 2 * size, size)


def each(start, stop, body):
    def step(index, carry):
        body(index)
        return carry

    lax.fori_loop(start, stop, step, 0)


def rows(start, size, step=16):
    return pl.ds(pl.multiple_of(start, step), size)


def dot(left, right):
    return jnp.dot(left, right, preferred_element_type=F32)


def dot_nt(left, right):
    return lax.dot_general(left, right, (((1,), (1,)), ((), ())), preferred_element_type=F32)


def dot_tn(left, right):
    return lax.dot_general(left, right, (((0,), (0,)), ((), ())), preferred_element_type=F32)


def fused_kernel(
    owner,
    latent_t,
    query_nope_in,
    query_rope_in,
    key_weight_in,
    value_weight_in,
    saved_in,
    output_grad_in,
    grad_nope,
    grad_rope,
    weight_all,
    latent_out,
    query_nope,
    query_rope,
    key_weight,
    value_weight,
    saved,
    output_grad,
    load_sem,
    keys,
    query_t,
    absorbed,
    grad_out_t,
    grad_out,
    delta,
    weights,
    prob_grad,
    score_low,
    probs_low,
    tops,
    sums,
    query_grad,
    weight_part,
    wa_in,
    wb_in,
    wa_sum,
    wb_sum,
    wa_near,
    wb_near,
    part,
    pair,
    ring,
    mine,
    y_in,
    z_in,
    y_sum,
    z_sum,
    y_last,
    z_last,
    near_y_send,
    near_y_recv,
    near_z_send,
    near_z_recv,
    ring_send,
    ring_recv,
    pass_send,
    pass_recv,
    wy_send,
    wy_recv,
    wz_send,
    wz_recv,
    pair_send,
    pair_recv,
    x_send,
    x_recv,
    ly_send,
    ly_recv,
    lz_send,
    lz_recv,
    head_send,
    head_recv,
):
    heads = query_nope.shape[1] // NOPE
    count = heads * TOK
    scale = (NOPE + ROPE) ** -0.5
    log2_scale = scale * math.log2(math.e)
    half = keys.shape[1] // 2
    chunks = keys.shape[0]

    ctx, head = lax.axis_index("ctx"), lax.axis_index("head")
    y, zh = ctx // NZH, lax.rem(ctx, NZH)
    zl = head // (2 * NX)
    x = lax.rem(head // 2, NX)
    core = lax.rem(head, 2)
    z = 2 * zh + zl
    turn = 1 - 2 * core
    sibling = device(y, zh, zl, x, 1 - core)
    heads_all = 4 * NX

    def y_peer(where):
        return device(where, zh, zl, x, core)

    def z_peer(where):
        return device(y, where // 2, lax.rem(where, 2), x, core)

    def zh_peer(where):
        return device(y, where, zl, x, core)

    def x_peer(where):
        return device(y, zh, zl, where, core)

    loads = []
    for source, dest in (
        (query_nope_in, query_nope),
        (key_weight_in, key_weight),
        (query_rope_in, query_rope),
        (value_weight_in, value_weight),
        (output_grad_in, output_grad),
        (saved_in, saved),
    ):
        loads.append(pltpu.make_async_copy(source, dest, load_sem.at[len(loads)]))
        loads[-1].start()

    latent = latent_t[...].astype(F32).T.astype(BF16)
    column = lax.broadcasted_iota(jnp.int32, (16, BLOCKS), 1)
    for side in range(2):
        mark = jnp.where(column == owner[side], 1.0, 0.0).astype(BF16)
        for piece in range(4):
            start = side * 64 + piece * 16
            if piece < 2:
                where, spot = y, rows(side * half + zh * 32 + piece * 16, 16)
            else:
                where, spot = NY + 2 * zh + piece - 2, rows(side * half + y * 16, 16)
            keys[where, spot, : LATENT + ROPE] = latent[start : start + 16, :]
            keys[where, spot, LATENT + ROPE :] = mark

    barrier = pltpu.get_barrier_semaphore()

    def hail(target):
        pl.semaphore_signal(barrier, inc=1, device_id=target, device_id_type=pl.DeviceIdType.MESH)

    each(1, NY, lambda d: hail(y_peer(wrap(y + d, NY))))
    each(1, NZ, lambda d: hail(z_peer(wrap(z + d, NZ))))
    each(1, heads_all, lambda d: hail((ctx, wrap(head + d, heads_all))))
    pl.semaphore_wait(barrier, NY - 1 + NZ - 1 + heads_all - 1)

    def near_y(d, spot):
        region = keys.at[NY + z, rows(core * half + spot * 16, 16)]
        return copy_to(region, region, near_y_send.at[d - 1], near_y_recv.at[d - 1], y_peer(wrap(y + d, NY)))

    def near_z(d, spot):
        region = keys.at[y, rows(core * half + spot * 32, 32, 32)]
        return copy_to(region, region, near_z_send.at[d - 1], near_z_recv.at[d - 1], zh_peer(wrap(zh + d, NZH)))

    each(1, NZH, lambda d: near_z(d, zh).start())
    each(1, NY, lambda d: near_y(d, y).start())

    for load in loads:
        load.wait()
    rope_t = query_rope[...].astype(F32).T.astype(BF16)
    block = lax.broadcasted_iota(jnp.int32, (BLOCKS, TOK), 0)
    token = lax.broadcasted_iota(jnp.int32, (BLOCKS, TOK), 1)
    limit = jnp.where(token < TOK // 2, owner[0], owner[1])
    bias = jnp.where(block <= limit, 0.0, HIDDEN).astype(BF16)
    for h in range(heads):
        cols = slice(h * NOPE, (h + 1) * NOPE)
        span = slice(h * TOK, (h + 1) * TOK)
        query, weight = query_nope[:, cols], key_weight[:, cols]
        query_t[:LATENT, span] = dot_nt(weight, query).astype(BF16)
        query_t[LATENT : LATENT + ROPE, span] = rope_t[h * ROPE : (h + 1) * ROPE, :]
        query_t[LATENT + ROPE :, span] = bias
        grad_out_t[:, span] = dot_nt(value_weight[:, cols], output_grad[:, cols]).astype(BF16)

    places = ((y, NY, 0), (z, NZ, NY))

    def ring_target(axis, rel):
        way = turn if rel == 0 else -turn
        return y_peer(wrap(y + way, NY)) if axis == 0 else z_peer(wrap(z + way, NZ))

    def ring_chunk(axis, rel, step):
        at, size, base = places[axis]
        way = turn if rel == 0 else -turn
        return base + wrap(at - way * step, size)

    def ring_copy(axis, rel, step, where):
        region = keys.at[where, rows(core * half, half, half)]
        return copy_to(
            region, region, ring_send.at[axis, rel, step], ring_recv.at[axis, rel, step], ring_target(axis, rel)
        )

    def pass_copy(axis, slot, where, side):
        region = keys.at[where, rows(side * half, half, half)]
        return copy_to(region, region, pass_send.at[axis, slot], pass_recv.at[axis, slot], sibling)

    def score(where):
        rows_in = keys[where]
        weights[where] = dot(rows_in, query_t[...])
        prob_grad[where] = dot(rows_in[:, :LATENT], grad_out_t[...])

        def hide(first, size, offset):
            for side in range(2):
                spot = rows(side * half + first, size)
                key_row = lax.broadcasted_iota(jnp.int32, (size, count), 0) + offset
                query_row = lax.rem(lax.broadcasted_iota(jnp.int32, (size, count), 1), TOK) - side * 64
                later = (query_row >= 0) & (query_row < 64) & (key_row > query_row)
                weights[where, spot, :] = jnp.where(later, HIDDEN, weights[where, spot, :])

        @pl.when(where == y)
        def _():
            hide(zh * 32, 32, 0)

        low = where - NY - 2 * zh

        @pl.when((low >= 0) & (low < 2))
        def _():
            hide(y * 16, 16, 32 + low * 16)

        raw = weights[where]
        top = jnp.max(raw, axis=0, keepdims=True)
        raised = jnp.exp2((raw - top) * log2_scale)
        weights[where] = raised
        tops[where] = top
        sums[where] = jnp.sum(raised, axis=0, keepdims=True)

    each(1, NZH, lambda d: near_z(d, wrap(zh - d, NZH)).wait_recv())
    for rel in range(2):
        if rel == 0 or NY > 2:
            ring_copy(0, rel, 0, y).start()
    each(1, NY, lambda d: near_y(d, wrap(y - d, NY)).wait_recv())
    for rel in range(2):
        if rel == 0 or NZ > 2:
            ring_copy(1, rel, 0, NY + z).start()
    pass_copy(0, 0, y, core).start()
    pass_copy(1, 0, NY + z, core).start()

    for h in range(heads):
        cols = slice(h * NOPE, (h + 1) * NOPE)
        span = slice(h * TOK, (h + 1) * TOK)
        side, at = h // (heads // 2), h % (heads // 2)
        place = slice(at * NOPE, (at + 1) * NOPE)
        out = output_grad[:, cols]
        grads = dot_nt(out, value_weight[:, cols]).astype(BF16)
        grad_out[span, :] = grads
        held = saved[:, h * LATENT : (h + 1) * LATENT]
        product = grads.astype(F32) * held.astype(F32)
        delta[:, span] = jnp.sum(product.T, axis=0, keepdims=True)
        weight_part[0, side, :, place] = dot_tn(held, out).astype(BF16)
        absorbed[span, :] = dot_nt(query_nope[:, cols], key_weight[:, cols]).astype(BF16)

    pass_copy(0, 0, y, 1 - core).wait_recv()
    pass_copy(1, 0, NY + z, 1 - core).wait_recv()
    each(0, 2, lambda i: score(i * (NY + z) + (1 - i) * y))

    ra, rb, rp = LATENT // NY, LATENT // NZH, LATENT // (NY * NZH)

    def wy_copy(w, stage, d, src, dst):
        return copy_to(
            src, dst, wy_send.at[w, stage, d - 1], wy_recv.at[w, stage, d - 1], y_peer(wrap(y + d, NY))
        )

    def wz_copy(w, stage, d, src, dst):
        return copy_to(
            src, dst, wz_send.at[w, stage, d - 1], wz_recv.at[w, stage, d - 1], zh_peer(wrap(zh + d, NZH))
        )

    def a_first(w, d):
        return wy_copy(w, 0, d, weight_part.at[w, 0, rows(wrap(y + d, NY) * ra, ra)], wa_in.at[w, d - 1])

    def b_first(w, d):
        return wz_copy(w, 0, d, weight_part.at[w, 1, rows(wrap(zh + d, NZH) * rb, rb)], wb_in.at[w, d - 1])

    def a_second(w, d):
        return wz_copy(w, 1, d, wa_sum.at[w, rows(wrap(zh + d, NZH) * rp, rp)], wa_near.at[w, d - 1])

    def b_second(w, d):
        return wy_copy(w, 1, d, wb_sum.at[w, rows(wrap(y + d, NY) * rp, rp)], wb_near.at[w, d - 1])

    def a_third(w, d, where):
        region = weight_all.at[w, 0, rows(y * ra + where * rp, rp)]
        return wz_copy(w, 2, d, region, region)

    def b_third(w, d, where):
        region = weight_all.at[w, 1, rows(zh * rb + where * rp, rp)]
        return wy_copy(w, 2, d, region, region)

    def a_fourth(w, d, where):
        region = weight_all.at[w, 0, rows(where * ra, ra)]
        return wy_copy(w, 3, d, region, region)

    def b_fourth(w, d, where):
        region = weight_all.at[w, 1, rows(where * rb, rb)]
        return wz_copy(w, 3, d, region, region)

    def weight_first(w):
        each(1, NY, lambda d: a_first(w, d).start())
        each(1, NZH, lambda d: b_first(w, d).start())

    def weight_second(w):
        each(1, NY, lambda d: a_first(w, d).wait_recv())
        total = weight_part[w, 0, rows(y * ra, ra), :].astype(F32)
        for d in range(1, NY):
            total += wa_in[w, d - 1].astype(F32)
        wa_sum[w] = total.astype(BF16)
        each(1, NZH, lambda d: a_second(w, d).start())
        each(1, NZH, lambda d: b_first(w, d).wait_recv())
        total = weight_part[w, 1, rows(zh * rb, rb), :].astype(F32)
        for d in range(1, NZH):
            total += wb_in[w, d - 1].astype(F32)
        wb_sum[w] = total.astype(BF16)
        each(1, NY, lambda d: b_second(w, d).start())

    def weight_third(w):
        each(1, NZH, lambda d: a_second(w, d).wait_recv())
        total = wa_sum[w, rows(zh * rp, rp), :].astype(F32)
        for d in range(1, NZH):
            total += wa_near[w, d - 1].astype(F32)
        weight_all[w, 0, rows(y * ra + zh * rp, rp), :] = total.astype(BF16)
        each(1, NZH, lambda d: a_third(w, d, zh).start())
        each(1, NY, lambda d: b_second(w, d).wait_recv())
        total = wb_sum[w, rows(y * rp, rp), :].astype(F32)
        for d in range(1, NY):
            total += wb_near[w, d - 1].astype(F32)
        weight_all[w, 1, rows(zh * rb + y * rp, rp), :] = total.astype(BF16)
        each(1, NY, lambda d: b_third(w, d, y).start())

    def weight_fourth(w):
        each(1, NZH, lambda d: a_third(w, d, wrap(zh - d, NZH)).wait_recv())
        each(1, NY, lambda d: a_fourth(w, d, y).start())
        each(1, NY, lambda d: b_third(w, d, wrap(y - d, NY)).wait_recv())
        each(1, NZH, lambda d: b_fourth(w, d, zh).start())

    def weight_last(w):
        each(1, NY, lambda d: a_fourth(w, d, wrap(y - d, NY)).wait_recv())
        each(1, NZH, lambda d: b_fourth(w, d, wrap(zh - d, NZH)).wait_recv())

    def weight_sent(w):
        def over_y(d):
            a_first(w, d).wait_send()
            b_second(w, d).wait_send()
            b_third(w, d, y).wait_send()
            a_fourth(w, d, y).wait_send()

        def over_z(d):
            b_first(w, d).wait_send()
            a_second(w, d).wait_send()
            a_third(w, d, zh).wait_send()
            b_fourth(w, d, zh).wait_send()

        each(1, NY, over_y)
        each(1, NZH, over_z)

    last = NY // 2 - 1
    for step in range(last):
        for rel in range(2):
            for axis in range(2):
                where = ring_chunk(axis, rel, step + 1)
                ring_copy(axis, rel, step, where).wait_recv()
                if rel == 0 or step + 1 < last:
                    ring_copy(axis, rel, step + 1, where).start()
                pass_copy(axis, 1 + 2 * step + rel, where, core).start()
        for rel in range(2):
            for axis in range(2):
                where = ring_chunk(axis, 1 - rel, step + 1)
                pass_copy(axis, 1 + 2 * step + rel, where, 1 - core).wait_recv()

        def arrived(i):
            axis, sign = i // 2, 1 - 2 * lax.rem(i, 2)
            score((1 - axis) * wrap(y - sign * (step + 1), NY) + axis * (NY + wrap(z - sign * (step + 1), NZ)))

        each(0, 4, arrived)
    for axis in range(2):
        where = ring_chunk(axis, 0, last + 1)
        ring_copy(axis, 0, last, where).wait_recv()
        pass_copy(axis, 1 + 2 * last, where, core).start()
    weight_first(0)
    for axis in range(2):
        pass_copy(axis, 1 + 2 * last, ring_chunk(axis, 0, last + 1), 1 - core).wait_recv()
    each(0, 2, lambda i: score((1 - i) * wrap(y + last + 1, NY) + i * (NY + wrap(z + last + 1, NZ))))

    highest = jnp.max(tops[...], axis=0)
    shares = jnp.exp2((tops[...] - highest[None]) * log2_scale)
    total = jnp.sum(shares * sums[...], axis=0)
    sums[...] = shares / total[None]
    query_grad[...] = jnp.zeros_like(query_grad)

    def gradients(where):
        probs = weights[where] * sums[where]
        grads = (probs * (prob_grad[where] - delta[...]) * scale).astype(BF16)
        score_low[where] = grads
        probs_low[where] = probs.astype(BF16)
        query_grad[...] += dot_tn(keys[where], grads)

    def key_weights():
        for h in range(heads):
            cols = slice(h * NOPE, (h + 1) * NOPE)
            span = slice(h * TOK, (h + 1) * TOK)
            side, at = h // (heads // 2), h % (heads // 2)
            place = slice(at * NOPE, (at + 1) * NOPE)
            value = dot(query_grad[:LATENT, span].astype(BF16), query_nope[:, cols])
            weight_part[1, side, :, place] = value.astype(BF16)

    wide = LATENT // NX
    size = chunks // GROUPS
    x_next, x_back = x_peer(wrap(x + turn, NX)), x_peer(wrap(x - turn, NX))

    def pair_copy(g):
        group = pl.ds(g * size, size)
        return copy_to(
            part.at[:, group, rows((1 - core) * half, half, half)],
            pair.at[:, group],
            pair_send.at[g],
            pair_recv.at[g],
            sibling,
        )

    def x_copy(kind, g):
        group = pl.ds(g * size, size)
        target = x_back if kind == 1 else x_next
        where = wrap(x + 2, NX) if kind == 0 else wrap(x - turn, NX) if kind == 1 else wrap(x + turn, NX)
        return copy_to(
            pair.at[where, group], ring.at[kind, group], x_send.at[kind, g], x_recv.at[kind, g], target
        )

    def terms(g):
        def one(i):
            where = g * size + i
            value = dot(score_low[where], absorbed[...]) + dot(probs_low[where], grad_out[...])
            for k in range(NX):
                part[k, where] = value[:, k * wide : (k + 1) * wide].astype(BF16)

        each(0, size, one)
        pair_copy(g).start()

    def pair_sum(g):
        pair_copy(g).wait_recv()

        def one(i):
            where = g * size + i
            for k in range(NX):
                value = part[k, where, rows(core * half, half, half), :].astype(F32) + pair[k, where].astype(F32)
                pair[k, where] = value.astype(BF16)

        each(0, size, one)
        x_copy(0, g).start()
        x_copy(1, g).start()

    def x_sum(g):
        x_copy(0, g).wait_recv()
        to = wrap(x + turn, NX)

        def one(i):
            where = g * size + i
            pair[to, where] = (pair[to, where].astype(F32) + ring[0, where].astype(F32)).astype(BF16)

        each(0, size, one)
        x_copy(2, g).start()

    def x_last(g):
        x_copy(1, g).wait_recv()
        x_copy(2, g).wait_recv()

        def one(i):
            where = g * size + i
            value = pair[x, where].astype(F32) + ring[1, where].astype(F32) + ring[2, where].astype(F32)
            mine[where] = value.astype(BF16)

        each(0, size, one)

    def ly_copy(stage, d, src, dst):
        return copy_to(src, dst, ly_send.at[stage, d - 1], ly_recv.at[stage, d - 1], y_peer(wrap(y + d, NY)))

    def lz_copy(stage, d, src, dst):
        return copy_to(src, dst, lz_send.at[stage, d - 1], lz_recv.at[stage, d - 1], z_peer(wrap(z + d, NZ)))

    def y_first(d):
        return ly_copy(0, d, mine.at[wrap(y + d, NY)], y_in.at[d - 1])

    def z_first(d):
        return lz_copy(0, d, mine.at[NY + wrap(z + d, NZ)], z_in.at[d - 1])

    def y_second(d):
        return ly_copy(1, d, z_sum.at[rows(wrap(y + d, NY) * 16, 16)], y_last.at[d - 1])

    def z_second(d):
        return lz_copy(1, d, y_sum.at[rows(wrap(z + d, NZ) * 16, 16)], z_last.at[d - 1])

    def send_on(g):
        def to_y(d):
            @pl.when(wrap(y + d, NY) // size == g)
            def _():
                y_first(d).start()

        def to_z(d):
            @pl.when((NY + wrap(z + d, NZ)) // size == g)
            def _():
                z_first(d).start()

        if g < GROUPS // 2:
            each(1, NY, to_y)
        else:
            each(1, NZ, to_z)

    def head_copy(d, who):
        region = latent_out.at[lax.rem(who, 2), who // (2 * NX), lax.rem(who // 2, NX)]
        return copy_to(
            region, region, head_send.at[d - 1], head_recv.at[d - 1], (ctx, wrap(head + d, heads_all))
        )

    def grads_of(g):
        each(g * size, (g + 1) * size, gradients)

    grads_of(0)
    terms(0)
    grads_of(1)
    pair_sum(0)
    terms(1)
    weight_second(0)
    grads_of(2)
    pair_sum(1)
    grads_of(3)
    key_weights()
    weight_first(1)
    x_sum(0)
    terms(2)
    weight_third(0)
    terms(3)
    pair_sum(2)
    x_sum(1)
    x_last(0)
    send_on(0)
    pair_sum(3)
    x_sum(2)
    weight_second(1)
    x_last(1)
    send_on(1)
    weight_fourth(0)
    for h in range(heads):
        cols = slice(h * NOPE, (h + 1) * NOPE)
        span = slice(h * TOK, (h + 1) * TOK)
        grad_nope[:, cols] = dot_tn(query_grad[:LATENT, span].astype(BF16), key_weight[:, cols]).astype(BF16)
    x_sum(3)
    x_last(2)
    send_on(2)
    rope_grad = jnp.concatenate(
        [query_grad[LATENT : LATENT + ROPE, h * TOK : (h + 1) * TOK] for h in range(heads)], axis=0
    )
    grad_rope[...] = rope_grad.T.astype(BF16)
    x_last(3)
    send_on(3)
    weight_third(1)

    each(1, NY, lambda d: y_first(d).wait_recv())
    total = mine[y].astype(F32)
    for d in range(1, NY):
        total += y_in[d - 1].astype(F32)
    y_sum[...] = total.astype(BF16)
    each(1, NZ, lambda d: z_second(d).start())
    each(1, NZ, lambda d: z_first(d).wait_recv())
    total = mine[NY + z].astype(F32)
    for d in range(1, NZ):
        total += z_in[d - 1].astype(F32)
    z_sum[...] = total.astype(BF16)
    each(1, NY, lambda d: y_second(d).start())
    each(1, NZ, lambda d: z_second(d).wait_recv())
    total = y_sum[rows(z * 16, 16), :].astype(F32)
    for d in range(1, NZ):
        total += z_last[d - 1].astype(F32)
    latent_out[core, zl, x, 0] = total.astype(BF16)
    weight_fourth(1)
    each(1, NY, lambda d: y_second(d).wait_recv())
    total = z_sum[rows(y * 16, 16), :].astype(F32)
    for d in range(1, NY):
        total += y_last[d - 1].astype(F32)
    latent_out[core, zl, x, 1] = total.astype(BF16)
    each(1, heads_all, lambda d: head_copy(d, head).start())
    weight_last(0)

    weight_last(1)
    each(1, NZH, lambda d: near_z(d, zh).wait_send())
    each(1, NY, lambda d: near_y(d, y).wait_send())
    for axis in range(2):
        for rel in range(2):
            for step in range(last + 1 - rel):
                ring_copy(axis, rel, step, ring_chunk(axis, rel, step)).wait_send()
        pass_copy(axis, 0, y if axis == 0 else NY + z, core).wait_send()
        for step in range(last + 1):
            for rel in range(2 if step < last else 1):
                pass_copy(axis, 1 + 2 * step + rel, ring_chunk(axis, rel, step + 1), core).wait_send()
    weight_sent(0)
    weight_sent(1)
    for g in range(GROUPS):
        pair_copy(g).wait_send()
        for kind in range(3):
            x_copy(kind, g).wait_send()

    def sent_y(d):
        y_first(d).wait_send()
        y_second(d).wait_send()

    def sent_z(d):
        z_first(d).wait_send()
        z_second(d).wait_send()

    each(1, NY, sent_y)
    each(1, NZ, sent_z)
    each(1, heads_all, lambda d: head_copy(d, wrap(head - d, heads_all)).wait_recv())
    each(1, heads_all, lambda d: head_copy(d, head).wait_send())


def fused(owner, latent_t, *inputs):
    query_nope, query_rope = inputs[:2]
    heads = query_nope.shape[1] // NOPE
    count = heads * TOK
    half = NZH * 32
    chunks = NY + NZ
    wide = LATENT // NX
    cols = count // 2
    ra, rb, rp = LATENT // NY, LATENT // NZH, LATENT // (NY * NZH)
    vmem = pl.BlockSpec(memory_space=pltpu.VMEM)
    dma = pltpu.SemaphoreType.DMA
    hold = pltpu.VMEM

    def sems(*shape):
        return [dma(shape), dma(shape)]

    return pl.pallas_call(
        fused_kernel,
        out_shape=(
            jax.ShapeDtypeStruct(query_nope.shape, BF16),
            jax.ShapeDtypeStruct(query_rope.shape, BF16),
            jax.ShapeDtypeStruct((2, 2, LATENT, cols), BF16),
            jax.ShapeDtypeStruct((2, 2, NX, 2, 16, wide), BF16),
        ),
        in_specs=[pl.BlockSpec(memory_space=pltpu.SMEM), vmem] + [pl.BlockSpec(memory_space=pl.ANY)] * 6,
        out_specs=(vmem,) * 4,
        scratch_shapes=[hold(array.shape, BF16) for array in inputs]
        + [
            dma((len(inputs),)),
            hold((chunks, 2 * half, WIDE), BF16),
            hold((WIDE, count), BF16),
            hold((count, LATENT), BF16),
            hold((LATENT, count), BF16),
            hold((count, LATENT), BF16),
            hold((1, count), F32),
            hold((chunks, 2 * half, count), F32),
            hold((chunks, 2 * half, count), F32),
            hold((chunks, 2 * half, count), BF16),
            hold((chunks, 2 * half, count), BF16),
            hold((chunks, 1, count), F32),
            hold((chunks, 1, count), F32),
            hold((WIDE, count), F32),
            hold((2, 2, LATENT, cols), BF16),
            hold((2, NY - 1, ra, cols), BF16),
            hold((2, NZH - 1, rb, cols), BF16),
            hold((2, ra, cols), BF16),
            hold((2, rb, cols), BF16),
            hold((2, NZH - 1, rp, cols), BF16),
            hold((2, NY - 1, rp, cols), BF16),
            hold((NX, chunks, 2 * half, wide), BF16),
            hold((NX, chunks, half, wide), BF16),
            hold((3, chunks, half, wide), BF16),
            hold((chunks, half, wide), BF16),
            hold((NY - 1, half, wide), BF16),
            hold((NZ - 1, half, wide), BF16),
            hold((half, wide), BF16),
            hold((half, wide), BF16),
            hold((NY - 1, 16, wide), BF16),
            hold((NZ - 1, 16, wide), BF16),
        ]
        + sems(NY - 1)
        + sems(NZH - 1)
        + sems(2, 2, NY // 2)
        + sems(2, NY)
        + sems(2, 4, NY - 1)
        + sems(2, 4, NZH - 1)
        + sems(GROUPS)
        + sems(3, GROUPS)
        + sems(2, NY - 1)
        + sems(2, NZ - 1)
        + sems(4 * NX - 1),
        compiler_params=pltpu.CompilerParams(
            collective_id=0, has_side_effects=True, vmem_limit_bytes=VMEM_LIMIT
        ),
        name="fused_grads",
    )(owner, latent_t, *inputs)


def finish_kernel(nope, rope, weight, latent, grad_nope, grad_rope, grad_latent, grad_key, grad_value):
    grad_nope[...] = nope[...]
    grad_rope[...] = rope[...]
    wide = LATENT // NX
    cols = weight.shape[3]
    for core in range(2):
        for low in range(2):
            for x in range(NX):
                for kind in range(2):
                    start = core * 64 + kind * 32 + low * 16
                    grad_latent[start : start + 16, x * wide : (x + 1) * wide] = latent[core, low, x, kind]
    for side in range(2):
        grad_value[:, side * cols : (side + 1) * cols] = weight[0, side].astype(F32)
        grad_key[:, side * cols : (side + 1) * cols] = weight[1, side].astype(F32)


def finish(nope, rope, weight, latent):
    vmem = pl.BlockSpec(memory_space=pltpu.VMEM)
    cols = 2 * weight.shape[3]
    return pl.pallas_call(
        finish_kernel,
        out_shape=(
            jax.ShapeDtypeStruct(nope.shape, BF16),
            jax.ShapeDtypeStruct(rope.shape, BF16),
            jax.ShapeDtypeStruct((TOK, LATENT), BF16),
            jax.ShapeDtypeStruct((LATENT, cols), F32),
            jax.ShapeDtypeStruct((LATENT, cols), F32),
        ),
        in_specs=[vmem] * 4,
        out_specs=(vmem,) * 5,
        compiler_params=pltpu.CompilerParams(vmem_limit_bytes=VMEM_LIMIT),
        name="finish",
    )(nope, rope, weight, latent)


def on_device(
    block_owner,
    query_nope,
    query_rope,
    latent_cache,
    key_up_weight,
    value_up_weight,
    saved_output,
    output_grad,
):
    return finish(
        *fused(
            block_owner,
            latent_cache.T,
            query_nope,
            query_rope,
            key_up_weight,
            value_up_weight,
            saved_output,
            output_grad,
        )
    )


def solution(mesh):
    return jax.shard_map(
        on_device,
        mesh=mesh,
        in_specs=(
            P("ctx"),
            P("ctx", "head"),
            P("ctx", "head"),
            P("ctx", None),
            P(None, "head"),
            P(None, "head"),
            P("ctx", "head"),
            P("ctx", "head"),
        ),
        out_specs=(
            P("ctx", "head"),
            P("ctx", "head"),
            P("ctx", None),
            P(None, "head"),
            P(None, "head"),
        ),
        check_vma=False,
    )
```

```python
import math

import jax
import jax.numpy as jnp
from jax import lax
from jax.experimental import pallas as pl
from jax.experimental.pallas import tpu as pltpu
from jax.sharding import PartitionSpec as P

LATENT = 512
ROPE = 64
NOPE = 128
NY, NZH, NX = 8, 4, 4
NZ = 2 * NZH
BLOCKS = 64
WIDE = LATENT + ROPE + BLOCKS
TOK = 128
GROUPS = 4
HIDDEN = -1e30
BF16 = jnp.bfloat16
F32 = jnp.float32
VMEM_LIMIT = 60 * 1024 * 1024


def device(y, zh, zl, x, core):
    return (y * NZH + zh, zl * (2 * NX) + x * 2 + core)


def copy_to(src, dst, send_sem, recv_sem, target):
    return pltpu.make_async_remote_copy(
        src_ref=src,
        dst_ref=dst,
        send_sem=send_sem,
        recv_sem=recv_sem,
        device_id=target,
        device_id_type=pl.DeviceIdType.MESH,
    )


def wrap(index, size):
    return lax.rem(index + 2 * size, size)


def each(start, stop, body):
    def step(index, carry):
        body(index)
        return carry

    lax.fori_loop(start, stop, step, 0)


def rows(start, size, step=16):
    return pl.ds(pl.multiple_of(start, step), size)


def dot(left, right):
    return jnp.dot(left, right, preferred_element_type=F32)


def dot_nt(left, right):
    return lax.dot_general(left, right, (((1,), (1,)), ((), ())), preferred_element_type=F32)


def dot_tn(left, right):
    return lax.dot_general(left, right, (((0,), (0,)), ((), ())), preferred_element_type=F32)


def fused_kernel(
    owner,
    latent_t,
    query_nope_in,
    query_rope_in,
    key_weight_in,
    value_weight_in,
    saved_in,
    output_grad_in,
    grad_nope,
    grad_rope,
    weight_all,
    latent_out,
    query_nope,
    query_rope,
    key_weight,
    value_weight,
    saved,
    output_grad,
    load_sem,
    keys,
    query_t,
    mixed,
    grad_out_t,
    delta,
    weights,
    prob_grad,
    low,
    tops,
    sums,
    query_grad,
    weight_part,
    wa_in,
    wb_in,
    wa_sum,
    wb_sum,
    wa_near,
    wb_near,
    part,
    pair,
    ring,
    mine,
    y_in,
    z_in,
    y_sum,
    z_sum,
    y_last,
    z_last,
    near_y_send,
    near_y_recv,
    near_z_send,
    near_z_recv,
    ring_send,
    ring_recv,
    pass_send,
    pass_recv,
    wy_send,
    wy_recv,
    wz_send,
    wz_recv,
    pair_send,
    pair_recv,
    x_send,
    x_recv,
    ly_send,
    ly_recv,
    lz_send,
    lz_recv,
    head_send,
    head_recv,
):
    heads = query_nope.shape[1] // NOPE
    count = heads * TOK
    scale = (NOPE + ROPE) ** -0.5
    log2_scale = scale * math.log2(math.e)
    half = keys.shape[1] // 2
    chunks = keys.shape[0]

    ctx, head = lax.axis_index("ctx"), lax.axis_index("head")
    y, zh = ctx // NZH, lax.rem(ctx, NZH)
    zl = head // (2 * NX)
    x = lax.rem(head // 2, NX)
    core = lax.rem(head, 2)
    z = 2 * zh + zl
    turn = 1 - 2 * core
    sibling = device(y, zh, zl, x, 1 - core)
    heads_all = 4 * NX

    def y_peer(where):
        return device(where, zh, zl, x, core)

    def z_peer(where):
        return device(y, where // 2, lax.rem(where, 2), x, core)

    def zh_peer(where):
        return device(y, where, zl, x, core)

    def x_peer(where):
        return device(y, zh, zl, where, core)

    loads = []
    for source, dest in (
        (query_nope_in, query_nope),
        (key_weight_in, key_weight),
        (query_rope_in, query_rope),
        (value_weight_in, value_weight),
        (output_grad_in, output_grad),
        (saved_in, saved),
    ):
        loads.append(pltpu.make_async_copy(source, dest, load_sem.at[len(loads)]))
        loads[-1].start()

    latent = latent_t[...].astype(F32).T.astype(BF16)
    column = lax.broadcasted_iota(jnp.int32, (16, BLOCKS), 1)
    for side in range(2):
        mark = jnp.where(column == owner[side], 1.0, 0.0).astype(BF16)
        for piece in range(4):
            start = side * 64 + piece * 16
            if piece < 2:
                where, spot = y, rows(side * half + zh * 32 + piece * 16, 16)
            else:
                where, spot = NY + 2 * zh + piece - 2, rows(side * half + y * 16, 16)
            keys[where, spot, : LATENT + ROPE] = latent[start : start + 16, :]
            keys[where, spot, LATENT + ROPE :] = mark

    barrier = pltpu.get_barrier_semaphore()

    def hail(target):
        pl.semaphore_signal(barrier, inc=1, device_id=target, device_id_type=pl.DeviceIdType.MESH)

    each(1, NY, lambda d: hail(y_peer(wrap(y + d, NY))))
    each(1, NZ, lambda d: hail(z_peer(wrap(z + d, NZ))))
    each(1, heads_all, lambda d: hail((ctx, wrap(head + d, heads_all))))
    pl.semaphore_wait(barrier, NY - 1 + NZ - 1 + heads_all - 1)

    def near_y(d, spot):
        region = keys.at[NY + z, rows(core * half + spot * 16, 16)]
        return copy_to(region, region, near_y_send.at[d - 1], near_y_recv.at[d - 1], y_peer(wrap(y + d, NY)))

    def near_z(d, spot):
        region = keys.at[y, rows(core * half + spot * 32, 32, 32)]
        return copy_to(region, region, near_z_send.at[d - 1], near_z_recv.at[d - 1], zh_peer(wrap(zh + d, NZH)))

    each(1, NZH, lambda d: near_z(d, zh).start())
    each(1, NY, lambda d: near_y(d, y).start())

    for load in loads:
        load.wait()
    rope_t = query_rope[...].astype(F32).T.astype(BF16)
    block = lax.broadcasted_iota(jnp.int32, (BLOCKS, TOK), 0)
    token = lax.broadcasted_iota(jnp.int32, (BLOCKS, TOK), 1)
    limit = jnp.where(token < TOK // 2, owner[0], owner[1])
    bias = jnp.where(block <= limit, 0.0, HIDDEN).astype(BF16)
    for h in range(heads):
        cols = slice(h * NOPE, (h + 1) * NOPE)
        span = slice(h * TOK, (h + 1) * TOK)
        query, weight = query_nope[:, cols], key_weight[:, cols]
        query_t[:LATENT, span] = dot_nt(weight, query).astype(BF16)
        query_t[LATENT : LATENT + ROPE, span] = rope_t[h * ROPE : (h + 1) * ROPE, :]
        query_t[LATENT + ROPE :, span] = bias
        grad_out_t[:, span] = dot_nt(value_weight[:, cols], output_grad[:, cols]).astype(BF16)

    places = ((y, NY, 0), (z, NZ, NY))

    def ring_target(axis, rel):
        way = turn if rel == 0 else -turn
        return y_peer(wrap(y + way, NY)) if axis == 0 else z_peer(wrap(z + way, NZ))

    def ring_chunk(axis, rel, step):
        at, size, base = places[axis]
        way = turn if rel == 0 else -turn
        return base + wrap(at - way * step, size)

    def ring_copy(axis, rel, step, where):
        region = keys.at[where, rows(core * half, half, half)]
        return copy_to(
            region, region, ring_send.at[axis, rel, step], ring_recv.at[axis, rel, step], ring_target(axis, rel)
        )

    def pass_copy(axis, slot, where, side):
        region = keys.at[where, rows(side * half, half, half)]
        return copy_to(region, region, pass_send.at[axis, slot], pass_recv.at[axis, slot], sibling)

    def score(where):
        rows_in = keys[where]
        weights[where] = dot(rows_in, query_t[...])
        prob_grad[where] = dot(rows_in[:, :LATENT], grad_out_t[...])

        def hide(first, size, offset):
            for side in range(2):
                spot = rows(side * half + first, size)
                key_row = lax.broadcasted_iota(jnp.int32, (size, count), 0) + offset
                query_row = lax.rem(lax.broadcasted_iota(jnp.int32, (size, count), 1), TOK) - side * 64
                later = (query_row >= 0) & (query_row < 64) & (key_row > query_row)
                weights[where, spot, :] = jnp.where(later, HIDDEN, weights[where, spot, :])

        @pl.when(where == y)
        def _():
            hide(zh * 32, 32, 0)

        low = where - NY - 2 * zh

        @pl.when((low >= 0) & (low < 2))
        def _():
            hide(y * 16, 16, 32 + low * 16)

        raw = weights[where]
        top = jnp.max(raw, axis=0, keepdims=True)
        raised = jnp.exp2((raw - top) * log2_scale)
        weights[where] = raised
        tops[where] = top
        sums[where] = jnp.sum(raised, axis=0, keepdims=True)
        prob_grad[where] = raised * ((prob_grad[where] - delta[...]) * scale)

    each(1, NZH, lambda d: near_z(d, wrap(zh - d, NZH)).wait_recv())
    for rel in range(2):
        if rel == 0 or NY > 2:
            ring_copy(0, rel, 0, y).start()
    each(1, NY, lambda d: near_y(d, wrap(y - d, NY)).wait_recv())
    for rel in range(2):
        if rel == 0 or NZ > 2:
            ring_copy(1, rel, 0, NY + z).start()
    pass_copy(0, 0, y, core).start()
    pass_copy(1, 0, NY + z, core).start()

    for h in range(heads):
        cols = slice(h * NOPE, (h + 1) * NOPE)
        span = slice(h * TOK, (h + 1) * TOK)
        side, at = h // (heads // 2), h % (heads // 2)
        place = slice(at * NOPE, (at + 1) * NOPE)
        out = output_grad[:, cols]
        grads = dot_nt(out, value_weight[:, cols]).astype(BF16)
        mixed[count + h * TOK : count + (h + 1) * TOK, :] = grads
        held = saved[:, h * LATENT : (h + 1) * LATENT]
        product = grads.astype(F32) * held.astype(F32)
        delta[:, span] = jnp.sum(product.T, axis=0, keepdims=True)
        weight_part[0, side, :, place] = dot_tn(held, out).astype(BF16)
        mixed[span, :] = dot_nt(query_nope[:, cols], key_weight[:, cols]).astype(BF16)

    pass_copy(0, 0, y, 1 - core).wait_recv()
    pass_copy(1, 0, NY + z, 1 - core).wait_recv()
    each(0, 2, lambda i: score(i * (NY + z) + (1 - i) * y))

    ra, rb, rp = LATENT // NY, LATENT // NZH, LATENT // (NY * NZH)

    def wy_copy(w, stage, d, src, dst):
        return copy_to(
            src, dst, wy_send.at[w, stage, d - 1], wy_recv.at[w, stage, d - 1], y_peer(wrap(y + d, NY))
        )

    def wz_copy(w, stage, d, src, dst):
        return copy_to(
            src, dst, wz_send.at[w, stage, d - 1], wz_recv.at[w, stage, d - 1], zh_peer(wrap(zh + d, NZH))
        )

    def a_first(w, d):
        return wy_copy(w, 0, d, weight_part.at[w, 0, rows(wrap(y + d, NY) * ra, ra)], wa_in.at[w, d - 1])

    def b_first(w, d):
        return wz_copy(w, 0, d, weight_part.at[w, 1, rows(wrap(zh + d, NZH) * rb, rb)], wb_in.at[w, d - 1])

    def a_second(w, d):
        return wz_copy(w, 1, d, wa_sum.at[w, rows(wrap(zh + d, NZH) * rp, rp)], wa_near.at[w, d - 1])

    def b_second(w, d):
        return wy_copy(w, 1, d, wb_sum.at[w, rows(wrap(y + d, NY) * rp, rp)], wb_near.at[w, d - 1])

    def a_third(w, d, where):
        region = weight_all.at[w, 0, rows(y * ra + where * rp, rp)]
        return wz_copy(w, 2, d, region, region)

    def b_third(w, d, where):
        region = weight_all.at[w, 1, rows(zh * rb + where * rp, rp)]
        return wy_copy(w, 2, d, region, region)

    def a_fourth(w, d, where):
        region = weight_all.at[w, 0, rows(where * ra, ra)]
        return wy_copy(w, 3, d, region, region)

    def b_fourth(w, d, where):
        region = weight_all.at[w, 1, rows(where * rb, rb)]
        return wz_copy(w, 3, d, region, region)

    def weight_first(w):
        each(1, NY, lambda d: a_first(w, d).start())
        each(1, NZH, lambda d: b_first(w, d).start())

    def weight_second(w):
        each(1, NY, lambda d: a_first(w, d).wait_recv())
        total = weight_part[w, 0, rows(y * ra, ra), :].astype(F32)
        for d in range(1, NY):
            total += wa_in[w, d - 1].astype(F32)
        wa_sum[w] = total.astype(BF16)
        each(1, NZH, lambda d: a_second(w, d).start())
        each(1, NZH, lambda d: b_first(w, d).wait_recv())
        total = weight_part[w, 1, rows(zh * rb, rb), :].astype(F32)
        for d in range(1, NZH):
            total += wb_in[w, d - 1].astype(F32)
        wb_sum[w] = total.astype(BF16)
        each(1, NY, lambda d: b_second(w, d).start())

    def weight_third(w):
        each(1, NZH, lambda d: a_second(w, d).wait_recv())
        total = wa_sum[w, rows(zh * rp, rp), :].astype(F32)
        for d in range(1, NZH):
            total += wa_near[w, d - 1].astype(F32)
        weight_all[w, 0, rows(y * ra + zh * rp, rp), :] = total.astype(BF16)
        each(1, NZH, lambda d: a_third(w, d, zh).start())
        each(1, NY, lambda d: b_second(w, d).wait_recv())
        total = wb_sum[w, rows(y * rp, rp), :].astype(F32)
        for d in range(1, NY):
            total += wb_near[w, d - 1].astype(F32)
        weight_all[w, 1, rows(zh * rb + y * rp, rp), :] = total.astype(BF16)
        each(1, NY, lambda d: b_third(w, d, y).start())

    def weight_fourth(w):
        each(1, NZH, lambda d: a_third(w, d, wrap(zh - d, NZH)).wait_recv())
        each(1, NY, lambda d: a_fourth(w, d, y).start())
        each(1, NY, lambda d: b_third(w, d, wrap(y - d, NY)).wait_recv())
        each(1, NZH, lambda d: b_fourth(w, d, zh).start())

    def weight_last(w):
        each(1, NY, lambda d: a_fourth(w, d, wrap(y - d, NY)).wait_recv())
        each(1, NZH, lambda d: b_fourth(w, d, wrap(zh - d, NZH)).wait_recv())

    def weight_sent(w):
        def over_y(d):
            a_first(w, d).wait_send()
            b_second(w, d).wait_send()
            b_third(w, d, y).wait_send()
            a_fourth(w, d, y).wait_send()

        def over_z(d):
            b_first(w, d).wait_send()
            a_second(w, d).wait_send()
            a_third(w, d, zh).wait_send()
            b_fourth(w, d, zh).wait_send()

        each(1, NY, over_y)
        each(1, NZH, over_z)

    last = NY // 2 - 1
    for step in range(last):
        for rel in range(2):
            for axis in range(2):
                where = ring_chunk(axis, rel, step + 1)
                ring_copy(axis, rel, step, where).wait_recv()
                if rel == 0 or step + 1 < last:
                    ring_copy(axis, rel, step + 1, where).start()
                pass_copy(axis, 1 + 2 * step + rel, where, core).start()
        for rel in range(2):
            for axis in range(2):
                where = ring_chunk(axis, 1 - rel, step + 1)
                pass_copy(axis, 1 + 2 * step + rel, where, 1 - core).wait_recv()

        def arrived(i):
            axis, sign = i // 2, 1 - 2 * lax.rem(i, 2)
            score((1 - axis) * wrap(y - sign * (step + 1), NY) + axis * (NY + wrap(z - sign * (step + 1), NZ)))

        each(0, 4, arrived)
    for axis in range(2):
        where = ring_chunk(axis, 0, last + 1)
        ring_copy(axis, 0, last, where).wait_recv()
        pass_copy(axis, 1 + 2 * last, where, core).start()
    weight_first(0)
    for axis in range(2):
        pass_copy(axis, 1 + 2 * last, ring_chunk(axis, 0, last + 1), 1 - core).wait_recv()
    each(0, 2, lambda i: score((1 - i) * wrap(y + last + 1, NY) + i * (NY + wrap(z + last + 1, NZ))))

    highest = jnp.max(tops[...], axis=0)
    shares = jnp.exp2((tops[...] - highest[None]) * log2_scale)
    total = jnp.sum(shares * sums[...], axis=0)
    sums[...] = shares / total[None]
    query_grad[...] = jnp.zeros_like(query_grad)

    per_step = 4

    def gradients(index):
        span = pl.ds(index * per_step, per_step)
        share = sums[span]
        grads = (prob_grad[span] * share).astype(BF16)
        low[span, :, :count] = grads
        low[span, :, count:] = (weights[span] * share).astype(BF16)
        flat = per_step * 2 * half
        query_grad[...] += dot_tn(keys[span].reshape(flat, WIDE), grads.reshape(flat, count))

    def key_weights():
        for h in range(heads):
            cols = slice(h * NOPE, (h + 1) * NOPE)
            span = slice(h * TOK, (h + 1) * TOK)
            side, at = h // (heads // 2), h % (heads // 2)
            place = slice(at * NOPE, (at + 1) * NOPE)
            value = dot(query_grad[:LATENT, span].astype(BF16), query_nope[:, cols])
            weight_part[1, side, :, place] = value.astype(BF16)

    wide = LATENT // NX
    size = chunks // GROUPS
    x_next, x_back = x_peer(wrap(x + turn, NX)), x_peer(wrap(x - turn, NX))

    def pair_copy(g):
        group = pl.ds(g * size, size)
        return copy_to(
            part.at[:, group, rows((1 - core) * half, half, half)],
            pair.at[:, group],
            pair_send.at[g],
            pair_recv.at[g],
            sibling,
        )

    def x_copy(kind, g):
        group = pl.ds(g * size, size)
        target = x_back if kind == 1 else x_next
        where = wrap(x + 2, NX) if kind == 0 else wrap(x - turn, NX) if kind == 1 else wrap(x + turn, NX)
        return copy_to(
            pair.at[where, group], ring.at[kind, group], x_send.at[kind, g], x_recv.at[kind, g], target
        )

    def terms(g):
        def one(i):
            span = pl.ds(g * size + i * per_step, per_step)
            flat = per_step * 2 * half
            block = low[span].reshape(flat, 2 * count)
            value = (dot(block, mixed[...])).astype(BF16)
            for k in range(NX):
                part[k, span] = value[:, k * wide : (k + 1) * wide].reshape(per_step, 2 * half, wide)

        each(0, size // per_step, one)
        pair_copy(g).start()

    def pair_sum(g):
        pair_copy(g).wait_recv()

        def one(i):
            where = g * size + i
            for k in range(NX):
                value = part[k, where, rows(core * half, half, half), :].astype(F32) + pair[k, where].astype(F32)
                pair[k, where] = value.astype(BF16)

        each(0, size, one)
        x_copy(0, g).start()
        x_copy(1, g).start()

    def x_sum(g):
        x_copy(0, g).wait_recv()
        to = wrap(x + turn, NX)

        def one(i):
            where = g * size + i
            pair[to, where] = (pair[to, where].astype(F32) + ring[0, where].astype(F32)).astype(BF16)

        each(0, size, one)
        x_copy(2, g).start()

    def x_last(g):
        x_copy(1, g).wait_recv()
        x_copy(2, g).wait_recv()

        def one(i):
            where = g * size + i
            value = pair[x, where].astype(F32) + ring[1, where].astype(F32) + ring[2, where].astype(F32)
            mine[where] = value.astype(BF16)

        each(0, size, one)

    def ly_copy(stage, d, src, dst):
        return copy_to(src, dst, ly_send.at[stage, d - 1], ly_recv.at[stage, d - 1], y_peer(wrap(y + d, NY)))

    def lz_copy(stage, d, src, dst):
        return copy_to(src, dst, lz_send.at[stage, d - 1], lz_recv.at[stage, d - 1], z_peer(wrap(z + d, NZ)))

    def y_first(d):
        return ly_copy(0, d, mine.at[wrap(y + d, NY)], y_in.at[d - 1])

    def z_first(d):
        return lz_copy(0, d, mine.at[NY + wrap(z + d, NZ)], z_in.at[d - 1])

    def y_second(d):
        return ly_copy(1, d, z_sum.at[rows(wrap(y + d, NY) * 16, 16)], y_last.at[d - 1])

    def z_second(d):
        return lz_copy(1, d, y_sum.at[rows(wrap(z + d, NZ) * 16, 16)], z_last.at[d - 1])

    def send_on(g):
        def to_y(d):
            @pl.when(wrap(y + d, NY) // size == g)
            def _():
                y_first(d).start()

        def to_z(d):
            @pl.when((NY + wrap(z + d, NZ)) // size == g)
            def _():
                z_first(d).start()

        if g < GROUPS // 2:
            each(1, NY, to_y)
        else:
            each(1, NZ, to_z)

    def head_copy(d, who):
        region = latent_out.at[lax.rem(who, 2), who // (2 * NX), lax.rem(who // 2, NX)]
        return copy_to(
            region, region, head_send.at[d - 1], head_recv.at[d - 1], (ctx, wrap(head + d, heads_all))
        )

    def grads_of(g):
        each(g * size // per_step, (g + 1) * size // per_step, gradients)

    grads_of(0)
    terms(0)
    grads_of(1)
    pair_sum(0)
    terms(1)
    weight_second(0)
    grads_of(2)
    pair_sum(1)
    grads_of(3)
    key_weights()
    weight_first(1)
    x_sum(0)
    terms(2)
    weight_third(0)
    terms(3)
    pair_sum(2)
    x_sum(1)
    x_last(0)
    send_on(0)
    pair_sum(3)
    each(1, NZH, lambda d: near_z(d, zh).wait_send())
    each(1, NY, lambda d: near_y(d, y).wait_send())
    for axis in range(2):
        for rel in range(2):
            for step in range(last + 1 - rel):
                ring_copy(axis, rel, step, ring_chunk(axis, rel, step)).wait_send()
        pass_copy(axis, 0, y if axis == 0 else NY + z, core).wait_send()
        for step in range(last + 1):
            for rel in range(2 if step < last else 1):
                pass_copy(axis, 1 + 2 * step + rel, ring_chunk(axis, rel, step + 1), core).wait_send()
    x_sum(2)
    weight_second(1)
    x_last(1)
    send_on(1)
    weight_fourth(0)
    for h in range(heads):
        cols = slice(h * NOPE, (h + 1) * NOPE)
        span = slice(h * TOK, (h + 1) * TOK)
        grad_nope[:, cols] = dot_tn(query_grad[:LATENT, span].astype(BF16), key_weight[:, cols]).astype(BF16)
    x_sum(3)
    x_last(2)
    send_on(2)
    rope_grad = jnp.concatenate(
        [query_grad[LATENT : LATENT + ROPE, h * TOK : (h + 1) * TOK] for h in range(heads)], axis=0
    )
    grad_rope[...] = rope_grad.T.astype(BF16)
    x_last(3)
    send_on(3)
    weight_third(1)
    for g in range(GROUPS):
        pair_copy(g).wait_send()
        for kind in range(3):
            x_copy(kind, g).wait_send()


    each(1, NY, lambda d: y_first(d).wait_recv())
    total = mine[y].astype(F32)
    for d in range(1, NY):
        total += y_in[d - 1].astype(F32)
    y_sum[...] = total.astype(BF16)
    each(1, NZ, lambda d: z_second(d).start())
    each(1, NZ, lambda d: z_first(d).wait_recv())
    total = mine[NY + z].astype(F32)
    for d in range(1, NZ):
        total += z_in[d - 1].astype(F32)
    z_sum[...] = total.astype(BF16)
    each(1, NY, lambda d: y_second(d).start())
    each(1, NZ, lambda d: z_second(d).wait_recv())
    total = y_sum[rows(z * 16, 16), :].astype(F32)
    for d in range(1, NZ):
        total += z_last[d - 1].astype(F32)
    latent_out[core, zl, x, 0] = total.astype(BF16)
    weight_fourth(1)
    each(1, NY, lambda d: y_second(d).wait_recv())
    total = z_sum[rows(y * 16, 16), :].astype(F32)
    for d in range(1, NY):
        total += y_last[d - 1].astype(F32)
    latent_out[core, zl, x, 1] = total.astype(BF16)
    each(1, heads_all, lambda d: head_copy(d, head).start())
    weight_last(0)

    weight_last(1)
    weight_sent(0)
    weight_sent(1)
    def sent_y(d):
        y_first(d).wait_send()
        y_second(d).wait_send()

    def sent_z(d):
        z_first(d).wait_send()
        z_second(d).wait_send()

    each(1, NY, sent_y)
    each(1, NZ, sent_z)
    each(1, heads_all, lambda d: head_copy(d, wrap(head - d, heads_all)).wait_recv())
    each(1, heads_all, lambda d: head_copy(d, head).wait_send())


def fused(owner, latent_t, *inputs):
    query_nope, query_rope = inputs[:2]
    heads = query_nope.shape[1] // NOPE
    count = heads * TOK
    half = NZH * 32
    chunks = NY + NZ
    wide = LATENT // NX
    cols = count // 2
    ra, rb, rp = LATENT // NY, LATENT // NZH, LATENT // (NY * NZH)
    vmem = pl.BlockSpec(memory_space=pltpu.VMEM)
    dma = pltpu.SemaphoreType.DMA
    hold = pltpu.VMEM

    def sems(*shape):
        return [dma(shape), dma(shape)]

    return pl.pallas_call(
        fused_kernel,
        out_shape=(
            jax.ShapeDtypeStruct(query_nope.shape, BF16),
            jax.ShapeDtypeStruct(query_rope.shape, BF16),
            jax.ShapeDtypeStruct((2, 2, LATENT, cols), BF16),
            jax.ShapeDtypeStruct((2, 2, NX, 2, 16, wide), BF16),
        ),
        in_specs=[pl.BlockSpec(memory_space=pltpu.SMEM), vmem] + [pl.BlockSpec(memory_space=pl.ANY)] * 6,
        out_specs=(vmem,) * 4,
        scratch_shapes=[hold(array.shape, BF16) for array in inputs]
        + [
            dma((len(inputs),)),
            hold((chunks, 2 * half, WIDE), BF16),
            hold((WIDE, count), BF16),
            hold((2 * count, LATENT), BF16),
            hold((LATENT, count), BF16),
            hold((1, count), F32),
            hold((chunks, 2 * half, count), F32),
            hold((chunks, 2 * half, count), F32),
            hold((chunks, 2 * half, 2 * count), BF16),
            hold((chunks, 1, count), F32),
            hold((chunks, 1, count), F32),
            hold((WIDE, count), F32),
            hold((2, 2, LATENT, cols), BF16),
            hold((2, NY - 1, ra, cols), BF16),
            hold((2, NZH - 1, rb, cols), BF16),
            hold((2, ra, cols), BF16),
            hold((2, rb, cols), BF16),
            hold((2, NZH - 1, rp, cols), BF16),
            hold((2, NY - 1, rp, cols), BF16),
            hold((NX, chunks, 2 * half, wide), BF16),
            hold((NX, chunks, half, wide), BF16),
            hold((3, chunks, half, wide), BF16),
            hold((chunks, half, wide), BF16),
            hold((NY - 1, half, wide), BF16),
            hold((NZ - 1, half, wide), BF16),
            hold((half, wide), BF16),
            hold((half, wide), BF16),
            hold((NY - 1, 16, wide), BF16),
            hold((NZ - 1, 16, wide), BF16),
        ]
        + sems(NY - 1)
        + sems(NZH - 1)
        + sems(2, 2, NY // 2)
        + sems(2, NY)
        + sems(2, 4, NY - 1)
        + sems(2, 4, NZH - 1)
        + sems(GROUPS)
        + sems(3, GROUPS)
        + sems(2, NY - 1)
        + sems(2, NZ - 1)
        + sems(4 * NX - 1),
        compiler_params=pltpu.CompilerParams(
            collective_id=0, has_side_effects=True, vmem_limit_bytes=VMEM_LIMIT
        ),
        name="fused_grads",
    )(owner, latent_t, *inputs)


def finish_kernel(nope, rope, weight, latent, grad_nope, grad_rope, grad_latent, grad_key, grad_value):
    grad_nope[...] = nope[...]
    grad_rope[...] = rope[...]
    wide = LATENT // NX
    cols = weight.shape[3]
    for core in range(2):
        for low in range(2):
            for x in range(NX):
                for kind in range(2):
                    start = core * 64 + kind * 32 + low * 16
                    grad_latent[start : start + 16, x * wide : (x + 1) * wide] = latent[core, low, x, kind]
    for side in range(2):
        grad_value[:, side * cols : (side + 1) * cols] = weight[0, side].astype(F32)
        grad_key[:, side * cols : (side + 1) * cols] = weight[1, side].astype(F32)


def finish(nope, rope, weight, latent):
    vmem = pl.BlockSpec(memory_space=pltpu.VMEM)
    cols = 2 * weight.shape[3]
    return pl.pallas_call(
        finish_kernel,
        out_shape=(
            jax.ShapeDtypeStruct(nope.shape, BF16),
            jax.ShapeDtypeStruct(rope.shape, BF16),
            jax.ShapeDtypeStruct((TOK, LATENT), BF16),
            jax.ShapeDtypeStruct((LATENT, cols), F32),
            jax.ShapeDtypeStruct((LATENT, cols), F32),
        ),
        in_specs=[vmem] * 4,
        out_specs=(vmem,) * 5,
        compiler_params=pltpu.CompilerParams(vmem_limit_bytes=VMEM_LIMIT),
        name="finish",
    )(nope, rope, weight, latent)


def on_device(
    block_owner,
    query_nope,
    query_rope,
    latent_cache,
    key_up_weight,
    value_up_weight,
    saved_output,
    output_grad,
):
    return finish(
        *fused(
            block_owner,
            latent_cache.T,
            query_nope,
            query_rope,
            key_up_weight,
            value_up_weight,
            saved_output,
            output_grad,
        )
    )


def solution(mesh):
    return jax.shard_map(
        on_device,
        mesh=mesh,
        in_specs=(
            P("ctx"),
            P("ctx", "head"),
            P("ctx", "head"),
            P("ctx", None),
            P(None, "head"),
            P(None, "head"),
            P("ctx", "head"),
            P("ctx", "head"),
        ),
        out_specs=(
            P("ctx", "head"),
            P("ctx", "head"),
            P("ctx", None),
            P(None, "head"),
            P(None, "head"),
        ),
        check_vma=False,
    )
```

```python
import math

import jax
import jax.numpy as jnp
from jax import lax
from jax.experimental import pallas as pl
from jax.experimental.pallas import tpu as pltpu
from jax.sharding import PartitionSpec as P

LATENT = 512
ROPE = 64
NOPE = 128
NY, NZH, NX = 8, 4, 4
NZ = 2 * NZH
BLOCKS = 64
WIDE = LATENT + ROPE + BLOCKS
TOK = 128
GROUPS = 4
HIDDEN = -1e30
BF16 = jnp.bfloat16
F32 = jnp.float32
VMEM_LIMIT = 60 * 1024 * 1024


def device(y, zh, zl, x, core):
    return (y * NZH + zh, zl * (2 * NX) + x * 2 + core)


def copy_to(src, dst, send_sem, recv_sem, target):
    return pltpu.make_async_remote_copy(
        src_ref=src,
        dst_ref=dst,
        send_sem=send_sem,
        recv_sem=recv_sem,
        device_id=target,
        device_id_type=pl.DeviceIdType.MESH,
    )


def wrap(index, size):
    return lax.rem(index + 2 * size, size)


def each(start, stop, body):
    def step(index, carry):
        body(index)
        return carry

    lax.fori_loop(start, stop, step, 0)


def rows(start, size, step=16):
    return pl.ds(pl.multiple_of(start, step), size)


def dot(left, right):
    return jnp.dot(left, right, preferred_element_type=F32)


def dot_nt(left, right):
    return lax.dot_general(left, right, (((1,), (1,)), ((), ())), preferred_element_type=F32)


def dot_tn(left, right):
    return lax.dot_general(left, right, (((0,), (0,)), ((), ())), preferred_element_type=F32)


def fused_kernel(
    owner,
    latent_t,
    query_nope_in,
    query_rope_in,
    key_weight_in,
    value_weight_in,
    saved_in,
    output_grad_in,
    grad_nope,
    grad_rope,
    weight_all,
    latent_out,
    query_nope,
    query_rope,
    key_weight,
    value_weight,
    saved,
    output_grad,
    load_sem,
    keys,
    query_t,
    mixed,
    grad_out_t,
    delta,
    weights,
    prob_grad,
    low,
    tops,
    sums,
    query_grad,
    weight_part,
    wa_in,
    wb_in,
    wa_sum,
    wb_sum,
    wa_near,
    wb_near,
    part,
    pair,
    ring,
    mine,
    y_in,
    z_in,
    y_sum,
    z_sum,
    y_last,
    z_last,
    near_y_send,
    near_y_recv,
    near_z_send,
    near_z_recv,
    ring_send,
    ring_recv,
    pass_send,
    pass_recv,
    wy_send,
    wy_recv,
    wz_send,
    wz_recv,
    pair_send,
    pair_recv,
    x_send,
    x_recv,
    ly_send,
    ly_recv,
    lz_send,
    lz_recv,
    head_send,
    head_recv,
):
    heads = query_nope.shape[1] // NOPE
    count = heads * TOK
    scale = (NOPE + ROPE) ** -0.5
    log2_scale = scale * math.log2(math.e)
    half = keys.shape[1] // 2
    chunks = keys.shape[0]

    ctx, head = lax.axis_index("ctx"), lax.axis_index("head")
    y, zh = ctx // NZH, lax.rem(ctx, NZH)
    zl = head // (2 * NX)
    x = lax.rem(head // 2, NX)
    core = lax.rem(head, 2)
    z = 2 * zh + zl
    turn = 1 - 2 * core
    sibling = device(y, zh, zl, x, 1 - core)
    heads_all = 4 * NX

    def y_peer(where):
        return device(where, zh, zl, x, core)

    def z_peer(where):
        return device(y, where // 2, lax.rem(where, 2), x, core)

    def zh_peer(where):
        return device(y, where, zl, x, core)

    def x_peer(where):
        return device(y, zh, zl, where, core)

    loads = []
    for source, dest in (
        (query_nope_in, query_nope),
        (key_weight_in, key_weight),
        (query_rope_in, query_rope),
        (value_weight_in, value_weight),
        (output_grad_in, output_grad),
        (saved_in, saved),
    ):
        loads.append(pltpu.make_async_copy(source, dest, load_sem.at[len(loads)]))
        loads[-1].start()

    latent = latent_t[...].astype(F32).T.astype(BF16)
    column = lax.broadcasted_iota(jnp.int32, (16, BLOCKS), 1)
    for side in range(2):
        mark = jnp.where(column == owner[side], 1.0, 0.0).astype(BF16)
        for piece in range(4):
            start = side * 64 + piece * 16
            if piece < 2:
                where, spot = y, rows(side * half + zh * 32 + piece * 16, 16)
            else:
                where, spot = NY + 2 * zh + piece - 2, rows(side * half + y * 16, 16)
            keys[where, spot, : LATENT + ROPE] = latent[start : start + 16, :]
            keys[where, spot, LATENT + ROPE :] = mark

    barrier = pltpu.get_barrier_semaphore()

    def hail(target):
        pl.semaphore_signal(barrier, inc=1, device_id=target, device_id_type=pl.DeviceIdType.MESH)

    each(1, NY, lambda d: hail(y_peer(wrap(y + d, NY))))
    each(1, NZ, lambda d: hail(z_peer(wrap(z + d, NZ))))
    each(1, heads_all, lambda d: hail((ctx, wrap(head + d, heads_all))))
    pl.semaphore_wait(barrier, NY - 1 + NZ - 1 + heads_all - 1)

    def near_y(d, spot):
        region = keys.at[NY + z, rows(core * half + spot * 16, 16)]
        return copy_to(region, region, near_y_send.at[d - 1], near_y_recv.at[d - 1], y_peer(wrap(y + d, NY)))

    def near_z(d, spot):
        region = keys.at[y, rows(core * half + spot * 32, 32, 32)]
        return copy_to(region, region, near_z_send.at[d - 1], near_z_recv.at[d - 1], zh_peer(wrap(zh + d, NZH)))

    each(1, NZH, lambda d: near_z(d, zh).start())
    each(1, NY, lambda d: near_y(d, y).start())

    for load in loads:
        load.wait()
    rope_t = query_rope[...].astype(F32).T.astype(BF16)
    block = lax.broadcasted_iota(jnp.int32, (BLOCKS, TOK), 0)
    token = lax.broadcasted_iota(jnp.int32, (BLOCKS, TOK), 1)
    limit = jnp.where(token < TOK // 2, owner[0], owner[1])
    bias = jnp.where(block <= limit, 0.0, HIDDEN).astype(BF16)
    for h in range(heads):
        cols = slice(h * NOPE, (h + 1) * NOPE)
        span = slice(h * TOK, (h + 1) * TOK)
        query, weight = query_nope[:, cols], key_weight[:, cols]
        query_t[:LATENT, span] = dot_nt(weight, query).astype(BF16)
        query_t[LATENT : LATENT + ROPE, span] = rope_t[h * ROPE : (h + 1) * ROPE, :]
        query_t[LATENT + ROPE :, span] = bias
        grad_out_t[:, span] = dot_nt(value_weight[:, cols], output_grad[:, cols]).astype(BF16)

    places = ((y, NY, 0), (z, NZ, NY))

    def ring_target(axis, rel):
        way = turn if rel == 0 else -turn
        return y_peer(wrap(y + way, NY)) if axis == 0 else z_peer(wrap(z + way, NZ))

    def ring_chunk(axis, rel, step):
        at, size, base = places[axis]
        way = turn if rel == 0 else -turn
        return base + wrap(at - way * step, size)

    def ring_copy(axis, rel, step, where):
        region = keys.at[where, rows(core * half, half, half)]
        return copy_to(
            region, region, ring_send.at[axis, rel, step], ring_recv.at[axis, rel, step], ring_target(axis, rel)
        )

    def pass_copy(axis, slot, where, side):
        region = keys.at[where, rows(side * half, half, half)]
        return copy_to(region, region, pass_send.at[axis, slot], pass_recv.at[axis, slot], sibling)

    def score(where):
        rows_in = keys[where]
        weights[where] = dot(rows_in, query_t[...])
        prob_grad[where] = dot(rows_in[:, :LATENT], grad_out_t[...])

        def hide(first, size, offset):
            for side in range(2):
                spot = rows(side * half + first, size)
                key_row = lax.broadcasted_iota(jnp.int32, (size, count), 0) + offset
                query_row = lax.rem(lax.broadcasted_iota(jnp.int32, (size, count), 1), TOK) - side * 64
                later = (query_row >= 0) & (query_row < 64) & (key_row > query_row)
                weights[where, spot, :] = jnp.where(later, HIDDEN, weights[where, spot, :])

        @pl.when(where == y)
        def _():
            hide(zh * 32, 32, 0)

        low = where - NY - 2 * zh

        @pl.when((low >= 0) & (low < 2))
        def _():
            hide(y * 16, 16, 32 + low * 16)

        raw = weights[where]
        top = jnp.max(raw, axis=0, keepdims=True)
        raised = jnp.exp2((raw - top) * log2_scale)
        weights[where] = raised
        tops[where] = top
        sums[where] = jnp.sum(raised, axis=0, keepdims=True)
        prob_grad[where] = raised * ((prob_grad[where] - delta[...]) * scale)

    each(1, NZH, lambda d: near_z(d, wrap(zh - d, NZH)).wait_recv())
    for rel in range(2):
        if rel == 0 or NY > 2:
            ring_copy(0, rel, 0, y).start()
    each(1, NY, lambda d: near_y(d, wrap(y - d, NY)).wait_recv())
    for rel in range(2):
        if rel == 0 or NZ > 2:
            ring_copy(1, rel, 0, NY + z).start()
    pass_copy(0, 0, y, core).start()
    pass_copy(1, 0, NY + z, core).start()

    for h in range(heads):
        cols = slice(h * NOPE, (h + 1) * NOPE)
        span = slice(h * TOK, (h + 1) * TOK)
        side, at = h // (heads // 2), h % (heads // 2)
        place = slice(at * NOPE, (at + 1) * NOPE)
        out = output_grad[:, cols]
        grads = dot_nt(out, value_weight[:, cols]).astype(BF16)
        mixed[count + h * TOK : count + (h + 1) * TOK, :] = grads
        held = saved[:, h * LATENT : (h + 1) * LATENT]
        product = grads.astype(F32) * held.astype(F32)
        delta[:, span] = jnp.sum(product.T, axis=0, keepdims=True)
        weight_part[0, side, :, place] = dot_tn(held, out).astype(BF16)
        mixed[span, :] = dot_nt(query_nope[:, cols], key_weight[:, cols]).astype(BF16)

    pass_copy(0, 0, y, 1 - core).wait_recv()
    pass_copy(1, 0, NY + z, 1 - core).wait_recv()
    each(0, 2, lambda i: score(i * (NY + z) + (1 - i) * y))

    ra, rb, rp = LATENT // NY, LATENT // NZH, LATENT // (NY * NZH)

    def wy_copy(w, stage, d, src, dst):
        return copy_to(
            src, dst, wy_send.at[w, stage, d - 1], wy_recv.at[w, stage, d - 1], y_peer(wrap(y + d, NY))
        )

    def wz_copy(w, stage, d, src, dst):
        return copy_to(
            src, dst, wz_send.at[w, stage, d - 1], wz_recv.at[w, stage, d - 1], zh_peer(wrap(zh + d, NZH))
        )

    def a_first(w, d):
        return wy_copy(w, 0, d, weight_part.at[w, 0, rows(wrap(y + d, NY) * ra, ra)], wa_in.at[w, d - 1])

    def b_first(w, d):
        return wz_copy(w, 0, d, weight_part.at[w, 1, rows(wrap(zh + d, NZH) * rb, rb)], wb_in.at[w, d - 1])

    def a_second(w, d):
        return wz_copy(w, 1, d, wa_sum.at[w, rows(wrap(zh + d, NZH) * rp, rp)], wa_near.at[w, d - 1])

    def b_second(w, d):
        return wy_copy(w, 1, d, wb_sum.at[w, rows(wrap(y + d, NY) * rp, rp)], wb_near.at[w, d - 1])

    def a_third(w, d, where):
        region = weight_all.at[w, 0, rows(y * ra + where * rp, rp)]
        return wz_copy(w, 2, d, region, region)

    def b_third(w, d, where):
        region = weight_all.at[w, 1, rows(zh * rb + where * rp, rp)]
        return wy_copy(w, 2, d, region, region)

    def a_fourth(w, d, where):
        region = weight_all.at[w, 0, rows(where * ra, ra)]
        return wy_copy(w, 3, d, region, region)

    def b_fourth(w, d, where):
        region = weight_all.at[w, 1, rows(where * rb, rb)]
        return wz_copy(w, 3, d, region, region)

    def weight_first(w):
        each(1, NY, lambda d: a_first(w, d).start())
        each(1, NZH, lambda d: b_first(w, d).start())

    def weight_second(w):
        each(1, NY, lambda d: a_first(w, d).wait_recv())
        total = weight_part[w, 0, rows(y * ra, ra), :].astype(F32)
        for d in range(1, NY):
            total += wa_in[w, d - 1].astype(F32)
        wa_sum[w] = total.astype(BF16)
        each(1, NZH, lambda d: a_second(w, d).start())
        each(1, NZH, lambda d: b_first(w, d).wait_recv())
        total = weight_part[w, 1, rows(zh * rb, rb), :].astype(F32)
        for d in range(1, NZH):
            total += wb_in[w, d - 1].astype(F32)
        wb_sum[w] = total.astype(BF16)
        each(1, NY, lambda d: b_second(w, d).start())

    def weight_third(w):
        each(1, NZH, lambda d: a_second(w, d).wait_recv())
        total = wa_sum[w, rows(zh * rp, rp), :].astype(F32)
        for d in range(1, NZH):
            total += wa_near[w, d - 1].astype(F32)
        weight_all[w, 0, rows(y * ra + zh * rp, rp), :] = total.astype(BF16)
        each(1, NZH, lambda d: a_third(w, d, zh).start())
        each(1, NY, lambda d: b_second(w, d).wait_recv())
        total = wb_sum[w, rows(y * rp, rp), :].astype(F32)
        for d in range(1, NY):
            total += wb_near[w, d - 1].astype(F32)
        weight_all[w, 1, rows(zh * rb + y * rp, rp), :] = total.astype(BF16)
        each(1, NY, lambda d: b_third(w, d, y).start())

    def weight_fourth(w):
        each(1, NZH, lambda d: a_third(w, d, wrap(zh - d, NZH)).wait_recv())
        each(1, NY, lambda d: a_fourth(w, d, y).start())
        each(1, NY, lambda d: b_third(w, d, wrap(y - d, NY)).wait_recv())
        each(1, NZH, lambda d: b_fourth(w, d, zh).start())

    def weight_last(w):
        each(1, NY, lambda d: a_fourth(w, d, wrap(y - d, NY)).wait_recv())
        each(1, NZH, lambda d: b_fourth(w, d, wrap(zh - d, NZH)).wait_recv())

    def weight_sent(w):
        def over_y(d):
            a_first(w, d).wait_send()
            b_second(w, d).wait_send()
            b_third(w, d, y).wait_send()
            a_fourth(w, d, y).wait_send()

        def over_z(d):
            b_first(w, d).wait_send()
            a_second(w, d).wait_send()
            a_third(w, d, zh).wait_send()
            b_fourth(w, d, zh).wait_send()

        each(1, NY, over_y)
        each(1, NZH, over_z)

    last = NY // 2 - 1
    for step in range(last):
        for rel in range(2):
            for axis in range(2):
                where = ring_chunk(axis, rel, step + 1)
                ring_copy(axis, rel, step, where).wait_recv()
                if rel == 0 or step + 1 < last:
                    ring_copy(axis, rel, step + 1, where).start()
                pass_copy(axis, 1 + 2 * step + rel, where, core).start()
        for rel in range(2):
            for axis in range(2):
                where = ring_chunk(axis, 1 - rel, step + 1)
                pass_copy(axis, 1 + 2 * step + rel, where, 1 - core).wait_recv()

        def arrived(i):
            axis, sign = i // 2, 1 - 2 * lax.rem(i, 2)
            score((1 - axis) * wrap(y - sign * (step + 1), NY) + axis * (NY + wrap(z - sign * (step + 1), NZ)))

        each(0, 4, arrived)
    for axis in range(2):
        where = ring_chunk(axis, 0, last + 1)
        ring_copy(axis, 0, last, where).wait_recv()
        pass_copy(axis, 1 + 2 * last, where, core).start()
    weight_first(0)
    for axis in range(2):
        pass_copy(axis, 1 + 2 * last, ring_chunk(axis, 0, last + 1), 1 - core).wait_recv()
    each(0, 2, lambda i: score((1 - i) * wrap(y + last + 1, NY) + i * (NY + wrap(z + last + 1, NZ))))

    highest = jnp.max(tops[...], axis=0)
    shares = jnp.exp2((tops[...] - highest[None]) * log2_scale)
    total = jnp.sum(shares * sums[...], axis=0)
    sums[...] = shares / total[None]
    query_grad[...] = jnp.zeros_like(query_grad)

    per_step = 4

    def gradients(index):
        span = pl.ds(index * per_step, per_step)
        share = sums[span]
        grads = (prob_grad[span] * share).astype(BF16)
        low[span, :, :count] = grads
        low[span, :, count:] = (weights[span] * share).astype(BF16)
        flat = per_step * 2 * half
        query_grad[...] += dot_tn(keys[span].reshape(flat, WIDE), grads.reshape(flat, count))

    def key_weights():
        for h in range(heads):
            cols = slice(h * NOPE, (h + 1) * NOPE)
            span = slice(h * TOK, (h + 1) * TOK)
            side, at = h // (heads // 2), h % (heads // 2)
            place = slice(at * NOPE, (at + 1) * NOPE)
            value = dot(query_grad[:LATENT, span].astype(BF16), query_nope[:, cols])
            weight_part[1, side, :, place] = value.astype(BF16)

    wide = LATENT // NX
    size = chunks // GROUPS
    x_next, x_back = x_peer(wrap(x + turn, NX)), x_peer(wrap(x - turn, NX))

    def pair_copy(g):
        group = pl.ds(g * size, size)
        return copy_to(
            part.at[:, group, rows((1 - core) * half, half, half)],
            pair.at[:, group],
            pair_send.at[g],
            pair_recv.at[g],
            sibling,
        )

    def x_copy(kind, g):
        group = pl.ds(g * size, size)
        target = x_back if kind == 1 else x_next
        where = wrap(x + 2, NX) if kind == 0 else wrap(x - turn, NX) if kind == 1 else wrap(x + turn, NX)
        return copy_to(
            pair.at[where, group], ring.at[kind, group], x_send.at[kind, g], x_recv.at[kind, g], target
        )

    def terms(g):
        def one(i):
            span = pl.ds(g * size + i * per_step, per_step)
            flat = per_step * 2 * half
            block = low[span].reshape(flat, 2 * count)
            value = (dot(block, mixed[...])).astype(BF16)
            for k in range(NX):
                part[k, span] = value[:, k * wide : (k + 1) * wide].reshape(per_step, 2 * half, wide)

        each(0, size // per_step, one)
        pair_copy(g).start()

    def pair_sum(g):
        pair_copy(g).wait_recv()

        def one(i):
            where = g * size + i
            for k in range(NX):
                value = part[k, where, rows(core * half, half, half), :].astype(F32) + pair[k, where].astype(F32)
                pair[k, where] = value.astype(BF16)

        each(0, size, one)
        x_copy(0, g).start()
        x_copy(1, g).start()

    def x_sum(g):
        x_copy(0, g).wait_recv()
        to = wrap(x + turn, NX)

        def one(i):
            where = g * size + i
            pair[to, where] = (pair[to, where].astype(F32) + ring[0, where].astype(F32)).astype(BF16)

        each(0, size, one)
        x_copy(2, g).start()

    def x_last(g):
        x_copy(1, g).wait_recv()
        x_copy(2, g).wait_recv()

        def one(i):
            where = g * size + i
            value = pair[x, where].astype(F32) + ring[1, where].astype(F32) + ring[2, where].astype(F32)
            mine[where] = value.astype(BF16)

        each(0, size, one)

    def ly_copy(stage, d, src, dst):
        return copy_to(src, dst, ly_send.at[stage, d - 1], ly_recv.at[stage, d - 1], y_peer(wrap(y + d, NY)))

    def lz_copy(stage, d, src, dst):
        return copy_to(src, dst, lz_send.at[stage, d - 1], lz_recv.at[stage, d - 1], z_peer(wrap(z + d, NZ)))

    def y_first(d):
        return ly_copy(0, d, mine.at[wrap(y + d, NY)], y_in.at[d - 1])

    def z_first(d):
        return lz_copy(0, d, mine.at[NY + wrap(z + d, NZ)], z_in.at[d - 1])

    def y_second(d):
        return ly_copy(1, d, z_sum.at[rows(wrap(y + d, NY) * 16, 16)], y_last.at[d - 1])

    def z_second(d):
        return lz_copy(1, d, y_sum.at[rows(wrap(z + d, NZ) * 16, 16)], z_last.at[d - 1])

    def send_on(g):
        def to_y(d):
            @pl.when(wrap(y + d, NY) // size == g)
            def _():
                y_first(d).start()

        def to_z(d):
            @pl.when((NY + wrap(z + d, NZ)) // size == g)
            def _():
                z_first(d).start()

        if g < GROUPS // 2:
            each(1, NY, to_y)
        else:
            each(1, NZ, to_z)

    def head_copy(d, who):
        region = latent_out.at[lax.rem(who, 2), who // (2 * NX), lax.rem(who // 2, NX)]
        return copy_to(
            region, region, head_send.at[d - 1], head_recv.at[d - 1], (ctx, wrap(head + d, heads_all))
        )

    def grads_of(g):
        each(g * size // per_step, (g + 1) * size // per_step, gradients)

    grads_of(0)
    terms(0)
    grads_of(1)
    pair_sum(0)
    terms(1)
    weight_second(0)
    grads_of(2)
    pair_sum(1)
    grads_of(3)
    key_weights()
    weight_first(1)
    x_sum(0)
    terms(2)
    weight_third(0)
    terms(3)
    pair_sum(2)
    x_sum(1)
    x_last(0)
    send_on(0)
    pair_sum(3)
    weight_second(1)
    each(1, NZH, lambda d: near_z(d, zh).wait_send())
    each(1, NY, lambda d: near_y(d, y).wait_send())
    for axis in range(2):
        for rel in range(2):
            for step in range(last + 1 - rel):
                ring_copy(axis, rel, step, ring_chunk(axis, rel, step)).wait_send()
        pass_copy(axis, 0, y if axis == 0 else NY + z, core).wait_send()
        for step in range(last + 1):
            for rel in range(2 if step < last else 1):
                pass_copy(axis, 1 + 2 * step + rel, ring_chunk(axis, rel, step + 1), core).wait_send()
    x_sum(2)
    x_last(1)
    send_on(1)
    weight_fourth(0)
    for h in range(heads):
        cols = slice(h * NOPE, (h + 1) * NOPE)
        span = slice(h * TOK, (h + 1) * TOK)
        grad_nope[:, cols] = dot_tn(query_grad[:LATENT, span].astype(BF16), key_weight[:, cols]).astype(BF16)
    x_sum(3)
    x_last(2)
    send_on(2)
    weight_third(1)
    rope_grad = jnp.concatenate(
        [query_grad[LATENT : LATENT + ROPE, h * TOK : (h + 1) * TOK] for h in range(heads)], axis=0
    )
    grad_rope[...] = rope_grad.T.astype(BF16)
    x_last(3)
    send_on(3)
    for g in range(GROUPS):
        pair_copy(g).wait_send()
        for kind in range(3):
            x_copy(kind, g).wait_send()


    each(1, NY, lambda d: y_first(d).wait_recv())
    total = mine[y].astype(F32)
    for d in range(1, NY):
        total += y_in[d - 1].astype(F32)
    y_sum[...] = total.astype(BF16)
    each(1, NZ, lambda d: z_second(d).start())
    each(1, NZ, lambda d: z_first(d).wait_recv())
    total = mine[NY + z].astype(F32)
    for d in range(1, NZ):
        total += z_in[d - 1].astype(F32)
    z_sum[...] = total.astype(BF16)
    each(1, NY, lambda d: y_second(d).start())
    weight_fourth(1)
    each(1, NZ, lambda d: z_second(d).wait_recv())
    total = y_sum[rows(z * 16, 16), :].astype(F32)
    for d in range(1, NZ):
        total += z_last[d - 1].astype(F32)
    latent_out[core, zl, x, 0] = total.astype(BF16)
    each(1, NY, lambda d: y_second(d).wait_recv())
    total = z_sum[rows(y * 16, 16), :].astype(F32)
    for d in range(1, NY):
        total += y_last[d - 1].astype(F32)
    latent_out[core, zl, x, 1] = total.astype(BF16)
    each(1, heads_all, lambda d: head_copy(d, head).start())
    weight_last(0)

    weight_last(1)
    weight_sent(0)
    weight_sent(1)
    def sent_y(d):
        y_first(d).wait_send()
        y_second(d).wait_send()

    def sent_z(d):
        z_first(d).wait_send()
        z_second(d).wait_send()

    each(1, NY, sent_y)
    each(1, NZ, sent_z)
    each(1, heads_all, lambda d: head_copy(d, wrap(head - d, heads_all)).wait_recv())
    each(1, heads_all, lambda d: head_copy(d, head).wait_send())


def fused(owner, latent_t, *inputs):
    query_nope, query_rope = inputs[:2]
    heads = query_nope.shape[1] // NOPE
    count = heads * TOK
    half = NZH * 32
    chunks = NY + NZ
    wide = LATENT // NX
    cols = count // 2
    ra, rb, rp = LATENT // NY, LATENT // NZH, LATENT // (NY * NZH)
    vmem = pl.BlockSpec(memory_space=pltpu.VMEM)
    dma = pltpu.SemaphoreType.DMA
    hold = pltpu.VMEM

    def sems(*shape):
        return [dma(shape), dma(shape)]

    return pl.pallas_call(
        fused_kernel,
        out_shape=(
            jax.ShapeDtypeStruct(query_nope.shape, BF16),
            jax.ShapeDtypeStruct(query_rope.shape, BF16),
            jax.ShapeDtypeStruct((2, 2, LATENT, cols), BF16),
            jax.ShapeDtypeStruct((2, 2, NX, 2, 16, wide), BF16),
        ),
        in_specs=[pl.BlockSpec(memory_space=pltpu.SMEM), vmem] + [pl.BlockSpec(memory_space=pl.ANY)] * 6,
        out_specs=(vmem,) * 4,
        scratch_shapes=[hold(array.shape, BF16) for array in inputs]
        + [
            dma((len(inputs),)),
            hold((chunks, 2 * half, WIDE), BF16),
            hold((WIDE, count), BF16),
            hold((2 * count, LATENT), BF16),
            hold((LATENT, count), BF16),
            hold((1, count), F32),
            hold((chunks, 2 * half, count), F32),
            hold((chunks, 2 * half, count), F32),
            hold((chunks, 2 * half, 2 * count), BF16),
            hold((chunks, 1, count), F32),
            hold((chunks, 1, count), F32),
            hold((WIDE, count), F32),
            hold((2, 2, LATENT, cols), BF16),
            hold((2, NY - 1, ra, cols), BF16),
            hold((2, NZH - 1, rb, cols), BF16),
            hold((2, ra, cols), BF16),
            hold((2, rb, cols), BF16),
            hold((2, NZH - 1, rp, cols), BF16),
            hold((2, NY - 1, rp, cols), BF16),
            hold((NX, chunks, 2 * half, wide), BF16),
            hold((NX, chunks, half, wide), BF16),
            hold((3, chunks, half, wide), BF16),
            hold((chunks, half, wide), BF16),
            hold((NY - 1, half, wide), BF16),
            hold((NZ - 1, half, wide), BF16),
            hold((half, wide), BF16),
            hold((half, wide), BF16),
            hold((NY - 1, 16, wide), BF16),
            hold((NZ - 1, 16, wide), BF16),
        ]
        + sems(NY - 1)
        + sems(NZH - 1)
        + sems(2, 2, NY // 2)
        + sems(2, NY)
        + sems(2, 4, NY - 1)
        + sems(2, 4, NZH - 1)
        + sems(GROUPS)
        + sems(3, GROUPS)
        + sems(2, NY - 1)
        + sems(2, NZ - 1)
        + sems(4 * NX - 1),
        compiler_params=pltpu.CompilerParams(
            collective_id=0, has_side_effects=True, vmem_limit_bytes=VMEM_LIMIT
        ),
        name="fused_grads",
    )(owner, latent_t, *inputs)


def finish_kernel(nope, rope, weight, latent, grad_nope, grad_rope, grad_latent, grad_key, grad_value):
    grad_nope[...] = nope[...]
    grad_rope[...] = rope[...]
    wide = LATENT // NX
    cols = weight.shape[3]
    for core in range(2):
        for low in range(2):
            for x in range(NX):
                for kind in range(2):
                    start = core * 64 + kind * 32 + low * 16
                    grad_latent[start : start + 16, x * wide : (x + 1) * wide] = latent[core, low, x, kind]
    for side in range(2):
        grad_value[:, side * cols : (side + 1) * cols] = weight[0, side].astype(F32)
        grad_key[:, side * cols : (side + 1) * cols] = weight[1, side].astype(F32)


def finish(nope, rope, weight, latent):
    vmem = pl.BlockSpec(memory_space=pltpu.VMEM)
    cols = 2 * weight.shape[3]
    return pl.pallas_call(
        finish_kernel,
        out_shape=(
            jax.ShapeDtypeStruct(nope.shape, BF16),
            jax.ShapeDtypeStruct(rope.shape, BF16),
            jax.ShapeDtypeStruct((TOK, LATENT), BF16),
            jax.ShapeDtypeStruct((LATENT, cols), F32),
            jax.ShapeDtypeStruct((LATENT, cols), F32),
        ),
        in_specs=[vmem] * 4,
        out_specs=(vmem,) * 5,
        compiler_params=pltpu.CompilerParams(vmem_limit_bytes=VMEM_LIMIT),
        name="finish",
    )(nope, rope, weight, latent)


def on_device(
    block_owner,
    query_nope,
    query_rope,
    latent_cache,
    key_up_weight,
    value_up_weight,
    saved_output,
    output_grad,
):
    return finish(
        *fused(
            block_owner,
            latent_cache.T,
            query_nope,
            query_rope,
            key_up_weight,
            value_up_weight,
            saved_output,
            output_grad,
        )
    )


def solution(mesh):
    return jax.shard_map(
        on_device,
        mesh=mesh,
        in_specs=(
            P("ctx"),
            P("ctx", "head"),
            P("ctx", "head"),
            P("ctx", None),
            P(None, "head"),
            P(None, "head"),
            P("ctx", "head"),
            P("ctx", "head"),
        ),
        out_specs=(
            P("ctx", "head"),
            P("ctx", "head"),
            P("ctx", None),
            P(None, "head"),
            P(None, "head"),
        ),
        check_vma=False,
    )
```

```python
import math

import jax
import jax.numpy as jnp
from jax import lax
from jax.experimental import pallas as pl
from jax.experimental.pallas import tpu as pltpu
from jax.sharding import PartitionSpec as P

LATENT = 512
ROPE = 64
NOPE = 128
NY, NZH, NX = 8, 4, 4
NZ = 2 * NZH
BLOCKS = 64
WIDE = LATENT + ROPE + BLOCKS
TOK = 128
GROUPS = 4
HIDDEN = -1e30
BF16 = jnp.bfloat16
F32 = jnp.float32
VMEM_LIMIT = 60 * 1024 * 1024


def device(y, zh, zl, x, core):
    return (y * NZH + zh, zl * (2 * NX) + x * 2 + core)


def copy_to(src, dst, send_sem, recv_sem, target):
    return pltpu.make_async_remote_copy(
        src_ref=src,
        dst_ref=dst,
        send_sem=send_sem,
        recv_sem=recv_sem,
        device_id=target,
        device_id_type=pl.DeviceIdType.MESH,
    )


def wrap(index, size):
    return lax.rem(index + 2 * size, size)


def each(start, stop, body):
    def step(index, carry):
        body(index)
        return carry

    lax.fori_loop(start, stop, step, 0)


def rows(start, size, step=16):
    return pl.ds(pl.multiple_of(start, step), size)


def dot(left, right):
    return jnp.dot(left, right, preferred_element_type=F32)


def dot_nt(left, right):
    return lax.dot_general(left, right, (((1,), (1,)), ((), ())), preferred_element_type=F32)


def dot_tn(left, right):
    return lax.dot_general(left, right, (((0,), (0,)), ((), ())), preferred_element_type=F32)


def fused_kernel(
    owner,
    latent_t,
    query_nope_in,
    query_rope_in,
    key_weight_in,
    value_weight_in,
    saved_in,
    output_grad_in,
    grad_nope,
    grad_rope,
    weight_all,
    latent_out,
    query_nope,
    query_rope,
    key_weight,
    value_weight,
    saved,
    output_grad,
    load_sem,
    keys,
    query_t,
    mixed,
    grad_out_t,
    delta,
    weights,
    prob_grad,
    low,
    tops,
    sums,
    query_grad,
    weight_part,
    wa_in,
    wb_in,
    wa_sum,
    wb_sum,
    wa_near,
    wb_near,
    part,
    pair,
    ring,
    mine,
    y_in,
    z_in,
    y_sum,
    z_sum,
    y_last,
    z_last,
    near_y_send,
    near_y_recv,
    near_z_send,
    near_z_recv,
    ring_send,
    ring_recv,
    pass_send,
    pass_recv,
    wy_send,
    wy_recv,
    wz_send,
    wz_recv,
    pair_send,
    pair_recv,
    x_send,
    x_recv,
    ly_send,
    ly_recv,
    lz_send,
    lz_recv,
    head_send,
    head_recv,
):
    heads = query_nope.shape[1] // NOPE
    count = heads * TOK
    scale = (NOPE + ROPE) ** -0.5
    log2_scale = scale * math.log2(math.e)
    half = keys.shape[1] // 2
    chunks = keys.shape[0]

    ctx, head = lax.axis_index("ctx"), lax.axis_index("head")
    y, zh = ctx // NZH, lax.rem(ctx, NZH)
    zl = head // (2 * NX)
    x = lax.rem(head // 2, NX)
    core = lax.rem(head, 2)
    z = 2 * zh + zl
    turn = 1 - 2 * core
    sibling = device(y, zh, zl, x, 1 - core)
    heads_all = 4 * NX

    def y_peer(where):
        return device(where, zh, zl, x, core)

    def z_peer(where):
        return device(y, where // 2, lax.rem(where, 2), x, core)

    def zh_peer(where):
        return device(y, where, zl, x, core)

    def x_peer(where):
        return device(y, zh, zl, where, core)

    loads = []
    for source, dest in (
        (query_nope_in, query_nope),
        (key_weight_in, key_weight),
        (query_rope_in, query_rope),
        (value_weight_in, value_weight),
        (output_grad_in, output_grad),
        (saved_in, saved),
    ):
        loads.append(pltpu.make_async_copy(source, dest, load_sem.at[len(loads)]))
        loads[-1].start()

    latent = latent_t[...].astype(F32).T.astype(BF16)
    column = lax.broadcasted_iota(jnp.int32, (16, BLOCKS), 1)
    for side in range(2):
        mark = jnp.where(column == owner[side], 1.0, 0.0).astype(BF16)
        for piece in range(4):
            start = side * 64 + piece * 16
            if piece < 2:
                where, spot = y, rows(side * half + zh * 32 + piece * 16, 16)
            else:
                where, spot = NY + 2 * zh + piece - 2, rows(side * half + y * 16, 16)
            keys[where, spot, : LATENT + ROPE] = latent[start : start + 16, :]
            keys[where, spot, LATENT + ROPE :] = mark

    barrier = pltpu.get_barrier_semaphore()

    def hail(target):
        pl.semaphore_signal(barrier, inc=1, device_id=target, device_id_type=pl.DeviceIdType.MESH)

    each(1, NY, lambda d: hail(y_peer(wrap(y + d, NY))))
    each(1, NZ, lambda d: hail(z_peer(wrap(z + d, NZ))))
    each(1, heads_all, lambda d: hail((ctx, wrap(head + d, heads_all))))
    pl.semaphore_wait(barrier, NY - 1 + NZ - 1 + heads_all - 1)

    def near_y(d, spot):
        region = keys.at[NY + z, rows(core * half + spot * 16, 16)]
        return copy_to(region, region, near_y_send.at[d - 1], near_y_recv.at[d - 1], y_peer(wrap(y + d, NY)))

    def near_z(d, spot):
        region = keys.at[y, rows(core * half + spot * 32, 32, 32)]
        return copy_to(region, region, near_z_send.at[d - 1], near_z_recv.at[d - 1], zh_peer(wrap(zh + d, NZH)))

    each(1, NZH, lambda d: near_z(d, zh).start())
    each(1, NY, lambda d: near_y(d, y).start())

    for load in loads:
        load.wait()
    rope_t = query_rope[...].astype(F32).T.astype(BF16)
    block = lax.broadcasted_iota(jnp.int32, (BLOCKS, TOK), 0)
    token = lax.broadcasted_iota(jnp.int32, (BLOCKS, TOK), 1)
    limit = jnp.where(token < TOK // 2, owner[0], owner[1])
    bias = jnp.where(block <= limit, 0.0, HIDDEN).astype(BF16)
    for h in range(heads):
        cols = slice(h * NOPE, (h + 1) * NOPE)
        span = slice(h * TOK, (h + 1) * TOK)
        query, weight = query_nope[:, cols], key_weight[:, cols]
        query_t[:LATENT, span] = dot_nt(weight, query).astype(BF16)
        query_t[LATENT : LATENT + ROPE, span] = rope_t[h * ROPE : (h + 1) * ROPE, :]
        query_t[LATENT + ROPE :, span] = bias
        grad_out_t[:, span] = dot_nt(value_weight[:, cols], output_grad[:, cols]).astype(BF16)

    places = ((y, NY, 0), (z, NZ, NY))

    def ring_target(axis, rel):
        way = turn if rel == 0 else -turn
        return y_peer(wrap(y + way, NY)) if axis == 0 else z_peer(wrap(z + way, NZ))

    def ring_chunk(axis, rel, step):
        at, size, base = places[axis]
        way = turn if rel == 0 else -turn
        return base + wrap(at - way * step, size)

    def ring_copy(axis, rel, step, where):
        region = keys.at[where, rows(core * half, half, half)]
        return copy_to(
            region, region, ring_send.at[axis, rel, step], ring_recv.at[axis, rel, step], ring_target(axis, rel)
        )

    def pass_copy(axis, slot, where, side):
        region = keys.at[where, rows(side * half, half, half)]
        return copy_to(region, region, pass_send.at[axis, slot], pass_recv.at[axis, slot], sibling)

    def score(where):
        rows_in = keys[where]
        weights[where] = dot(rows_in, query_t[...])
        prob_grad[where] = dot(rows_in[:, :LATENT], grad_out_t[...])

        def hide(first, size, offset):
            for side in range(2):
                spot = rows(side * half + first, size)
                key_row = lax.broadcasted_iota(jnp.int32, (size, count), 0) + offset
                query_row = lax.rem(lax.broadcasted_iota(jnp.int32, (size, count), 1), TOK) - side * 64
                later = (query_row >= 0) & (query_row < 64) & (key_row > query_row)
                weights[where, spot, :] = jnp.where(later, HIDDEN, weights[where, spot, :])

        @pl.when(where == y)
        def _():
            hide(zh * 32, 32, 0)

        low = where - NY - 2 * zh

        @pl.when((low >= 0) & (low < 2))
        def _():
            hide(y * 16, 16, 32 + low * 16)

        raw = weights[where]
        top = jnp.max(raw, axis=0, keepdims=True)
        raised = jnp.exp2((raw - top) * log2_scale)
        weights[where] = raised
        tops[where] = top
        sums[where] = jnp.sum(raised, axis=0, keepdims=True)
        prob_grad[where] = raised * ((prob_grad[where] - delta[...]) * scale)

    each(1, NZH, lambda d: near_z(d, wrap(zh - d, NZH)).wait_recv())
    for rel in range(2):
        if rel == 0 or NY > 2:
            ring_copy(0, rel, 0, y).start()
    each(1, NY, lambda d: near_y(d, wrap(y - d, NY)).wait_recv())
    for rel in range(2):
        if rel == 0 or NZ > 2:
            ring_copy(1, rel, 0, NY + z).start()
    pass_copy(0, 0, y, core).start()
    pass_copy(1, 0, NY + z, core).start()

    for h in range(heads):
        cols = slice(h * NOPE, (h + 1) * NOPE)
        span = slice(h * TOK, (h + 1) * TOK)
        side, at = h // (heads // 2), h % (heads // 2)
        place = slice(at * NOPE, (at + 1) * NOPE)
        out = output_grad[:, cols]
        grads = dot_nt(out, value_weight[:, cols]).astype(BF16)
        mixed[count + h * TOK : count + (h + 1) * TOK, :] = grads
        held = saved[:, h * LATENT : (h + 1) * LATENT]
        product = grads.astype(F32) * held.astype(F32)
        delta[:, span] = jnp.sum(product.T, axis=0, keepdims=True)
        weight_part[0, side, :, place] = dot_tn(held, out).astype(BF16)
        mixed[span, :] = dot_nt(query_nope[:, cols], key_weight[:, cols]).astype(BF16)

    pass_copy(0, 0, y, 1 - core).wait_recv()
    pass_copy(1, 0, NY + z, 1 - core).wait_recv()
    each(0, 2, lambda i: score(i * (NY + z) + (1 - i) * y))

    ra, rb, rp = LATENT // NY, LATENT // NZH, LATENT // (NY * NZH)

    def wy_copy(w, stage, d, src, dst):
        return copy_to(
            src, dst, wy_send.at[w, stage, d - 1], wy_recv.at[w, stage, d - 1], y_peer(wrap(y + d, NY))
        )

    def wz_copy(w, stage, d, src, dst):
        return copy_to(
            src, dst, wz_send.at[w, stage, d - 1], wz_recv.at[w, stage, d - 1], zh_peer(wrap(zh + d, NZH))
        )

    def a_first(w, d):
        return wy_copy(w, 0, d, weight_part.at[w, 0, rows(wrap(y + d, NY) * ra, ra)], wa_in.at[w, d - 1])

    def b_first(w, d):
        return wz_copy(w, 0, d, weight_part.at[w, 1, rows(wrap(zh + d, NZH) * rb, rb)], wb_in.at[w, d - 1])

    def a_second(w, d):
        return wz_copy(w, 1, d, wa_sum.at[w, rows(wrap(zh + d, NZH) * rp, rp)], wa_near.at[w, d - 1])

    def b_second(w, d):
        return wy_copy(w, 1, d, wb_sum.at[w, rows(wrap(y + d, NY) * rp, rp)], wb_near.at[w, d - 1])

    def a_third(w, d, where):
        region = weight_all.at[w, 0, rows(y * ra + where * rp, rp)]
        return wz_copy(w, 2, d, region, region)

    def b_third(w, d, where):
        region = weight_all.at[w, 1, rows(zh * rb + where * rp, rp)]
        return wy_copy(w, 2, d, region, region)

    def a_fourth(w, d, where):
        region = weight_all.at[w, 0, rows(where * ra, ra)]
        return wy_copy(w, 3, d, region, region)

    def b_fourth(w, d, where):
        region = weight_all.at[w, 1, rows(where * rb, rb)]
        return wz_copy(w, 3, d, region, region)

    def weight_first(w):
        each(1, NY, lambda d: a_first(w, d).start())
        each(1, NZH, lambda d: b_first(w, d).start())

    def weight_second(w):
        each(1, NY, lambda d: a_first(w, d).wait_recv())
        total = weight_part[w, 0, rows(y * ra, ra), :].astype(F32)
        for d in range(1, NY):
            total += wa_in[w, d - 1].astype(F32)
        wa_sum[w] = total.astype(BF16)
        each(1, NZH, lambda d: a_second(w, d).start())
        each(1, NZH, lambda d: b_first(w, d).wait_recv())
        total = weight_part[w, 1, rows(zh * rb, rb), :].astype(F32)
        for d in range(1, NZH):
            total += wb_in[w, d - 1].astype(F32)
        wb_sum[w] = total.astype(BF16)
        each(1, NY, lambda d: b_second(w, d).start())

    def weight_third(w):
        each(1, NZH, lambda d: a_second(w, d).wait_recv())
        total = wa_sum[w, rows(zh * rp, rp), :].astype(F32)
        for d in range(1, NZH):
            total += wa_near[w, d - 1].astype(F32)
        weight_all[w, 0, rows(y * ra + zh * rp, rp), :] = total.astype(BF16)
        each(1, NZH, lambda d: a_third(w, d, zh).start())
        each(1, NY, lambda d: b_second(w, d).wait_recv())
        total = wb_sum[w, rows(y * rp, rp), :].astype(F32)
        for d in range(1, NY):
            total += wb_near[w, d - 1].astype(F32)
        weight_all[w, 1, rows(zh * rb + y * rp, rp), :] = total.astype(BF16)
        each(1, NY, lambda d: b_third(w, d, y).start())

    def weight_fourth(w):
        each(1, NZH, lambda d: a_third(w, d, wrap(zh - d, NZH)).wait_recv())
        each(1, NY, lambda d: a_fourth(w, d, y).start())
        each(1, NY, lambda d: b_third(w, d, wrap(y - d, NY)).wait_recv())
        each(1, NZH, lambda d: b_fourth(w, d, zh).start())

    def weight_last(w):
        each(1, NY, lambda d: a_fourth(w, d, wrap(y - d, NY)).wait_recv())
        each(1, NZH, lambda d: b_fourth(w, d, wrap(zh - d, NZH)).wait_recv())

    def weight_sent(w):
        def over_y(d):
            a_first(w, d).wait_send()
            b_second(w, d).wait_send()
            b_third(w, d, y).wait_send()
            a_fourth(w, d, y).wait_send()

        def over_z(d):
            b_first(w, d).wait_send()
            a_second(w, d).wait_send()
            a_third(w, d, zh).wait_send()
            b_fourth(w, d, zh).wait_send()

        each(1, NY, over_y)
        each(1, NZH, over_z)

    last = NY // 2 - 1
    for step in range(last):
        for rel in range(2):
            for axis in range(2):
                where = ring_chunk(axis, rel, step + 1)
                ring_copy(axis, rel, step, where).wait_recv()
                if rel == 0 or step + 1 < last:
                    ring_copy(axis, rel, step + 1, where).start()
                pass_copy(axis, 1 + 2 * step + rel, where, core).start()
        for rel in range(2):
            for axis in range(2):
                where = ring_chunk(axis, 1 - rel, step + 1)
                pass_copy(axis, 1 + 2 * step + rel, where, 1 - core).wait_recv()

        def arrived(i):
            axis, sign = i // 2, 1 - 2 * lax.rem(i, 2)
            score((1 - axis) * wrap(y - sign * (step + 1), NY) + axis * (NY + wrap(z - sign * (step + 1), NZ)))

        each(0, 4, arrived)
    for axis in range(2):
        where = ring_chunk(axis, 0, last + 1)
        ring_copy(axis, 0, last, where).wait_recv()
        pass_copy(axis, 1 + 2 * last, where, core).start()
    weight_first(0)
    for axis in range(2):
        pass_copy(axis, 1 + 2 * last, ring_chunk(axis, 0, last + 1), 1 - core).wait_recv()
    each(0, 2, lambda i: score((1 - i) * wrap(y + last + 1, NY) + i * (NY + wrap(z + last + 1, NZ))))

    highest = jnp.max(tops[...], axis=0)
    shares = jnp.exp2((tops[...] - highest[None]) * log2_scale)
    total = jnp.sum(shares * sums[...], axis=0)
    sums[...] = shares / total[None]
    query_grad[...] = jnp.zeros_like(query_grad)

    per_step = 4

    def gradients(index):
        span = pl.ds(index * per_step, per_step)
        share = sums[span]
        grads = (prob_grad[span] * share).astype(BF16)
        low[span, :, :count] = grads
        low[span, :, count:] = (weights[span] * share).astype(BF16)
        flat = per_step * 2 * half
        query_grad[...] += dot_tn(keys[span].reshape(flat, WIDE), grads.reshape(flat, count))

    def key_weights():
        for h in range(heads):
            cols = slice(h * NOPE, (h + 1) * NOPE)
            span = slice(h * TOK, (h + 1) * TOK)
            side, at = h // (heads // 2), h % (heads // 2)
            place = slice(at * NOPE, (at + 1) * NOPE)
            value = dot(query_grad[:LATENT, span].astype(BF16), query_nope[:, cols])
            weight_part[1, side, :, place] = value.astype(BF16)

    wide = LATENT // NX
    size = chunks // GROUPS
    x_next, x_back = x_peer(wrap(x + turn, NX)), x_peer(wrap(x - turn, NX))

    def pair_copy(g):
        group = pl.ds(g * size, size)
        return copy_to(
            part.at[:, group, rows((1 - core) * half, half, half)],
            pair.at[:, group],
            pair_send.at[g],
            pair_recv.at[g],
            sibling,
        )

    def x_copy(kind, g):
        group = pl.ds(g * size, size)
        target = x_back if kind == 1 else x_next
        where = wrap(x + 2, NX) if kind == 0 else wrap(x - turn, NX) if kind == 1 else wrap(x + turn, NX)
        return copy_to(
            pair.at[where, group], ring.at[kind, group], x_send.at[kind, g], x_recv.at[kind, g], target
        )

    def terms(g):
        def one(i):
            span = pl.ds(g * size + i * per_step, per_step)
            flat = per_step * 2 * half
            block = low[span].reshape(flat, 2 * count)
            value = (dot(block, mixed[...])).astype(BF16)
            for k in range(NX):
                part[k, span] = value[:, k * wide : (k + 1) * wide].reshape(per_step, 2 * half, wide)

        each(0, size // per_step, one)
        pair_copy(g).start()

    def pair_sum(g):
        pair_copy(g).wait_recv()

        def one(i):
            where = g * size + i
            for k in range(NX):
                value = part[k, where, rows(core * half, half, half), :].astype(F32) + pair[k, where].astype(F32)
                pair[k, where] = value.astype(BF16)

        each(0, size, one)
        x_copy(0, g).start()
        x_copy(1, g).start()

    def x_sum(g):
        x_copy(0, g).wait_recv()
        to = wrap(x + turn, NX)

        def one(i):
            where = g * size + i
            pair[to, where] = (pair[to, where].astype(F32) + ring[0, where].astype(F32)).astype(BF16)

        each(0, size, one)
        x_copy(2, g).start()

    def x_last(g):
        x_copy(1, g).wait_recv()
        x_copy(2, g).wait_recv()

        def one(i):
            where = g * size + i
            value = pair[x, where].astype(F32) + ring[1, where].astype(F32) + ring[2, where].astype(F32)
            mine[where] = value.astype(BF16)

        each(0, size, one)

    def ly_copy(stage, d, src, dst):
        return copy_to(src, dst, ly_send.at[stage, d - 1], ly_recv.at[stage, d - 1], y_peer(wrap(y + d, NY)))

    def lz_copy(stage, d, src, dst):
        return copy_to(src, dst, lz_send.at[stage, d - 1], lz_recv.at[stage, d - 1], z_peer(wrap(z + d, NZ)))

    def y_first(d):
        return ly_copy(0, d, mine.at[wrap(y + d, NY)], y_in.at[d - 1])

    def z_first(d):
        return lz_copy(0, d, mine.at[NY + wrap(z + d, NZ)], z_in.at[d - 1])

    def y_second(d):
        return ly_copy(1, d, z_sum.at[rows(wrap(y + d, NY) * 16, 16)], y_last.at[d - 1])

    def z_second(d):
        return lz_copy(1, d, y_sum.at[rows(wrap(z + d, NZ) * 16, 16)], z_last.at[d - 1])

    def send_on(g):
        def to_y(d):
            @pl.when(wrap(y + d, NY) // size == g)
            def _():
                y_first(d).start()

        def to_z(d):
            @pl.when((NY + wrap(z + d, NZ)) // size == g)
            def _():
                z_first(d).start()

        if g < GROUPS // 2:
            each(1, NY, to_y)
        else:
            each(1, NZ, to_z)

    def head_copy(d, who):
        region = latent_out.at[lax.rem(who, 2), who // (2 * NX), lax.rem(who // 2, NX)]
        return copy_to(
            region, region, head_send.at[d - 1], head_recv.at[d - 1], (ctx, wrap(head + d, heads_all))
        )

    def grads_of(g):
        each(g * size // per_step, (g + 1) * size // per_step, gradients)

    grads_of(0)
    terms(0)
    grads_of(1)
    pair_sum(0)
    terms(1)
    weight_second(0)
    grads_of(2)
    pair_sum(1)
    grads_of(3)
    key_weights()
    weight_first(1)
    x_sum(0)
    terms(2)
    weight_third(0)
    terms(3)
    pair_sum(2)
    x_sum(1)
    x_last(0)
    send_on(0)
    pair_sum(3)
    weight_second(1)
    each(1, NZH, lambda d: near_z(d, zh).wait_send())
    each(1, NY, lambda d: near_y(d, y).wait_send())
    for axis in range(2):
        for rel in range(2):
            for step in range(last + 1 - rel):
                ring_copy(axis, rel, step, ring_chunk(axis, rel, step)).wait_send()
        pass_copy(axis, 0, y if axis == 0 else NY + z, core).wait_send()
        for step in range(last + 1):
            for rel in range(2 if step < last else 1):
                pass_copy(axis, 1 + 2 * step + rel, ring_chunk(axis, rel, step + 1), core).wait_send()
    x_sum(2)
    x_last(1)
    send_on(1)
    weight_fourth(0)
    for h in range(heads):
        cols = slice(h * NOPE, (h + 1) * NOPE)
        span = slice(h * TOK, (h + 1) * TOK)
        grad_nope[:, cols] = dot_tn(query_grad[:LATENT, span].astype(BF16), key_weight[:, cols]).astype(BF16)
    x_sum(3)
    x_last(2)
    send_on(2)
    weight_third(1)
    rope_grad = jnp.concatenate(
        [query_grad[LATENT : LATENT + ROPE, h * TOK : (h + 1) * TOK] for h in range(heads)], axis=0
    )
    grad_rope[...] = rope_grad.T.astype(BF16)
    x_last(3)
    send_on(3)
    for g in range(GROUPS):
        pair_copy(g).wait_send()
        for kind in range(3):
            x_copy(kind, g).wait_send()


    each(1, NY, lambda d: y_first(d).wait_recv())
    total = mine[y].astype(F32)
    for d in range(1, NY):
        total += y_in[d - 1].astype(F32)
    y_sum[...] = total.astype(BF16)
    each(1, NZ, lambda d: z_second(d).start())
    each(1, NZ, lambda d: z_first(d).wait_recv())
    total = mine[NY + z].astype(F32)
    for d in range(1, NZ):
        total += z_in[d - 1].astype(F32)
    z_sum[...] = total.astype(BF16)
    each(1, NY, lambda d: y_second(d).start())
    weight_fourth(1)
    weight_last(0)
    weight_sent(0)
    each(1, NY, lambda d: y_first(d).wait_send())
    each(1, NZ, lambda d: z_first(d).wait_send())
    each(1, NZ, lambda d: z_second(d).wait_recv())
    total = y_sum[rows(z * 16, 16), :].astype(F32)
    for d in range(1, NZ):
        total += z_last[d - 1].astype(F32)
    latent_out[core, zl, x, 0] = total.astype(BF16)
    each(1, NY, lambda d: y_second(d).wait_recv())
    total = z_sum[rows(y * 16, 16), :].astype(F32)
    for d in range(1, NY):
        total += y_last[d - 1].astype(F32)
    latent_out[core, zl, x, 1] = total.astype(BF16)
    each(1, heads_all, lambda d: head_copy(d, head).start())

    weight_last(1)
    weight_sent(1)
    def sent_y(d):
        y_second(d).wait_send()

    def sent_z(d):
        z_second(d).wait_send()

    each(1, NY, sent_y)
    each(1, NZ, sent_z)
    each(1, heads_all, lambda d: head_copy(d, wrap(head - d, heads_all)).wait_recv())
    each(1, heads_all, lambda d: head_copy(d, head).wait_send())


def fused(owner, latent_t, *inputs):
    query_nope, query_rope = inputs[:2]
    heads = query_nope.shape[1] // NOPE
    count = heads * TOK
    half = NZH * 32
    chunks = NY + NZ
    wide = LATENT // NX
    cols = count // 2
    ra, rb, rp = LATENT // NY, LATENT // NZH, LATENT // (NY * NZH)
    vmem = pl.BlockSpec(memory_space=pltpu.VMEM)
    dma = pltpu.SemaphoreType.DMA
    hold = pltpu.VMEM

    def sems(*shape):
        return [dma(shape), dma(shape)]

    return pl.pallas_call(
        fused_kernel,
        out_shape=(
            jax.ShapeDtypeStruct(query_nope.shape, BF16),
            jax.ShapeDtypeStruct(query_rope.shape, BF16),
            jax.ShapeDtypeStruct((2, 2, LATENT, cols), BF16),
            jax.ShapeDtypeStruct((2, 2, NX, 2, 16, wide), BF16),
        ),
        in_specs=[pl.BlockSpec(memory_space=pltpu.SMEM), vmem] + [pl.BlockSpec(memory_space=pl.ANY)] * 6,
        out_specs=(vmem,) * 4,
        scratch_shapes=[hold(array.shape, BF16) for array in inputs]
        + [
            dma((len(inputs),)),
            hold((chunks, 2 * half, WIDE), BF16),
            hold((WIDE, count), BF16),
            hold((2 * count, LATENT), BF16),
            hold((LATENT, count), BF16),
            hold((1, count), F32),
            hold((chunks, 2 * half, count), F32),
            hold((chunks, 2 * half, count), F32),
            hold((chunks, 2 * half, 2 * count), BF16),
            hold((chunks, 1, count), F32),
            hold((chunks, 1, count), F32),
            hold((WIDE, count), F32),
            hold((2, 2, LATENT, cols), BF16),
            hold((2, NY - 1, ra, cols), BF16),
            hold((2, NZH - 1, rb, cols), BF16),
            hold((2, ra, cols), BF16),
            hold((2, rb, cols), BF16),
            hold((2, NZH - 1, rp, cols), BF16),
            hold((2, NY - 1, rp, cols), BF16),
            hold((NX, chunks, 2 * half, wide), BF16),
            hold((NX, chunks, half, wide), BF16),
            hold((3, chunks, half, wide), BF16),
            hold((chunks, half, wide), BF16),
            hold((NY - 1, half, wide), BF16),
            hold((NZ - 1, half, wide), BF16),
            hold((half, wide), BF16),
            hold((half, wide), BF16),
            hold((NY - 1, 16, wide), BF16),
            hold((NZ - 1, 16, wide), BF16),
        ]
        + sems(NY - 1)
        + sems(NZH - 1)
        + sems(2, 2, NY // 2)
        + sems(2, NY)
        + sems(2, 4, NY - 1)
        + sems(2, 4, NZH - 1)
        + sems(GROUPS)
        + sems(3, GROUPS)
        + sems(2, NY - 1)
        + sems(2, NZ - 1)
        + sems(4 * NX - 1),
        compiler_params=pltpu.CompilerParams(
            collective_id=0, has_side_effects=True, vmem_limit_bytes=VMEM_LIMIT
        ),
        name="fused_grads",
    )(owner, latent_t, *inputs)


def finish_kernel(nope, rope, weight, latent, grad_nope, grad_rope, grad_latent, grad_key, grad_value):
    grad_nope[...] = nope[...]
    grad_rope[...] = rope[...]
    wide = LATENT // NX
    cols = weight.shape[3]
    for core in range(2):
        for low in range(2):
            for x in range(NX):
                for kind in range(2):
                    start = core * 64 + kind * 32 + low * 16
                    grad_latent[start : start + 16, x * wide : (x + 1) * wide] = latent[core, low, x, kind]
    for side in range(2):
        grad_value[:, side * cols : (side + 1) * cols] = weight[0, side].astype(F32)
        grad_key[:, side * cols : (side + 1) * cols] = weight[1, side].astype(F32)


def finish(nope, rope, weight, latent):
    vmem = pl.BlockSpec(memory_space=pltpu.VMEM)
    cols = 2 * weight.shape[3]
    return pl.pallas_call(
        finish_kernel,
        out_shape=(
            jax.ShapeDtypeStruct(nope.shape, BF16),
            jax.ShapeDtypeStruct(rope.shape, BF16),
            jax.ShapeDtypeStruct((TOK, LATENT), BF16),
            jax.ShapeDtypeStruct((LATENT, cols), F32),
            jax.ShapeDtypeStruct((LATENT, cols), F32),
        ),
        in_specs=[vmem] * 4,
        out_specs=(vmem,) * 5,
        compiler_params=pltpu.CompilerParams(vmem_limit_bytes=VMEM_LIMIT),
        name="finish",
    )(nope, rope, weight, latent)


def on_device(
    block_owner,
    query_nope,
    query_rope,
    latent_cache,
    key_up_weight,
    value_up_weight,
    saved_output,
    output_grad,
):
    return finish(
        *fused(
            block_owner,
            latent_cache.T,
            query_nope,
            query_rope,
            key_up_weight,
            value_up_weight,
            saved_output,
            output_grad,
        )
    )


def solution(mesh):
    return jax.shard_map(
        on_device,
        mesh=mesh,
        in_specs=(
            P("ctx"),
            P("ctx", "head"),
            P("ctx", "head"),
            P("ctx", None),
            P(None, "head"),
            P(None, "head"),
            P("ctx", "head"),
            P("ctx", "head"),
        ),
        out_specs=(
            P("ctx", "head"),
            P("ctx", "head"),
            P("ctx", None),
            P(None, "head"),
            P(None, "head"),
        ),
        check_vma=False,
    )
```
